256 devices in a mesh: ctx: 8 (over x, core), exp: 32 (over y, z).
Axes of the slice: x: 4, y: 4, z: 8, core: 2. Of those that a mesh axis runs over, the one named last changes fastest.
Arguments:
- tokens_in: bfloat16 [1024, 6144], P('ctx'), may hold values from -6 to 6
- queries: bfloat16 [1024, 8192], P('ctx', 'exp'), may hold values from -6 to 6
- keys: bfloat16 [1024, 8192], P('ctx', 'exp'), may hold values from -6 to 6
- values: bfloat16 [1024, 8192], P('ctx', 'exp'), may hold values from -6 to 6
- log_decay: float32 [64, 1024], P('exp', 'ctx'), may hold values from -1.3 to 0
- incoming_state: float32 [64, 128, 128], P('exp'), may hold values from -12 to 12
- attn_gain: float32 [8192], P('exp'), may hold values from 0.1 to 1.9
- w_out: bfloat16 [8192, 6144], P('exp'), may hold values from -0.0625 to 0.0625
- ffn_gain: float32 [6144], replicated, may hold values from 0.1 to 1.9
- router: bfloat16 [6144, 4], replicated, may hold values from -0.078125 to 0.078125
- expert_ids: int32 [1024, 2], P('ctx'), may hold values from 0 to 3, all different within a row; in each aligned block of 128 rows (0 to 127, 128 to 255, ...) at most 80 rows name the same one
- w_in: bfloat16 [2, 36864, 6144], P(None, ('exp', 'ctx')), may hold values from -0.078125 to 0.078125
- w_down: bfloat16 [36864, 6144], P(('exp', 'ctx')), may hold values from -0.0625 to 0.0625
Outputs:
- mixed: bfloat16 [1024, 6144], P('ctx', 'exp')
The draws below stay inside these ranges and needn't reach their ends.
Inputs may be any that keep to these rules, and one draw needn't show every extreme that they name: `expert_ids`: A token's two experts differ. Among the 128 tokens of one index of ctx no expert is named by more than 80 tokens, a bound that some block reaches of them.
All inputs are finite; a program needn't handle non-finite values.
Results may differ from the reference program's by a relative error of at most 0.027.
Values may be sent and summed in bfloat16 or wider, within the bound.
A program may use at most 128 MiB of HBM per device.

```python
import math
import jax
import jax.numpy as jnp
import numpy as np
from jax import lax

D = 6144
HEADS = 64
HD = 128
FF = 9216
E_WIN = 4
TOK_DEV = 128
TOKENS = 1024
CAP = 80
SLICE = 144


def draw_log_decay(key, part):
    key = jax.random.fold_in(key, 11)
    key_list = jax.random.split(key, 6)
    fast_share = 0.5
    fast = jax.random.uniform(key_list[0], (HEADS, 1)) < fast_share
    fast_rate = jnp.exp(jax.random.uniform(key_list[1], (HEADS, 1), minval=math.log(1.0 / 50.0), maxval=math.log(1.0 / 30.0)))
    slow_rate = jnp.exp(jax.random.uniform(key_list[2], (HEADS, 1), minval=math.log(0.05), maxval=math.log(0.6))) / TOKENS
    decay_rate = jnp.where(fast, fast_rate, slow_rate)
    coarse_estimate = jax.random.uniform(key_list[3], (HEADS, TOKENS), minval=0.5, maxval=1.5)
    slot_locations = jax.random.randint(key_list[4], (HEADS, 2), 0, TOKENS)
    balance_loss = jax.random.uniform(key_list[5], (HEADS, 2), minval=0.2, maxval=0.45)
    token_position = jnp.arange(TOKENS)[None, :, None]
    token_surge = jnp.sum(jnp.where(token_position == slot_locations[:, None, :], jnp.log(1.0 - balance_loss)[:, None, :], 0.0), axis=2)
    return (-decay_rate * coarse_estimate + token_surge).astype(jnp.float32)


def shard_levels(key, dims, cuts, least, largest):
    level, own = 1.0, jax.random.fold_in(key, 6)
    for dim, blocks in cuts:
        draws = jnp.exp(jax.random.uniform(jax.random.fold_in(own, dim), (blocks,), jnp.float32, least / len(cuts), largest / len(cuts)))
        level = level * jnp.repeat(draws, dims[dim] // blocks).reshape([-1 if axis == dim else 1 for axis in range(len(dims))])
    return level


def deal_out(stream_key, own, number, rows, amount, top, most, slope):
    ranking = jax.random.permutation(stream_key, amount)
    packed, ordinary = load_shares(amount, rows * top, most, slope, True), load_shares(amount, rows * top, most, slope, False)
    places = jnp.arange(amount)

    def named(lengths, offset_by):
        used = int((lengths > 0).sum())
        fixed = max(1, used // 4)
        shifted = fixed + (places - fixed + offset_by * (used - fixed)) % max(1, amount - fixed)
        return jnp.zeros((amount,), jnp.int32).at[ranking[jnp.where(places < fixed, places, shifted)]].set(jnp.asarray(lengths, jnp.int32))

    lengths = jnp.where(number % 4 == 0, named(packed, number // 4), named(ordinary, number - number // 4 - 1))
    mixed = jax.random.permutation(jax.random.fold_in(own, 3), amount)
    giver, receiver = mixed[0:amount // 2 * 2:2], mixed[1:amount // 2 * 2:2]
    margin = jnp.minimum(lengths[giver] - 1, most - lengths[receiver]) // 2
    margin = jnp.where((giver == ranking[0]) | (receiver == ranking[0]) | (lengths[receiver] == 0), 0, jnp.maximum(margin, 0))
    shifted = jax.random.randint(jax.random.fold_in(own, 4), (amount // 2,), 0, 1 << 20) % (margin + 1)
    lengths = lengths.at[giver].add(-shifted).at[receiver].add(shifted)
    members = jnp.searchsorted(jnp.cumsum(lengths), jnp.arange(rows * top), side="right").astype(jnp.int32)
    listing = members.reshape(top, rows).T
    listing = listing[jax.random.permutation(jax.random.fold_in(own, 1), rows)]
    offset_by = jax.random.randint(jax.random.fold_in(own, 2), (rows, 1), 0, top)
    return jnp.take_along_axis(listing, (jnp.arange(top)[None, :] + offset_by) % top, axis=1)


def load_shares(amount, total, reach, lean, full):
    loads = [(1 << 20) // math.isqrt(rank ** lean) + 1 for rank in range(1, amount + 1)]
    largest = reach if full else min(reach, max(-(-total // amount), total * loads[0] // sum(loads)))
    least = 1 if total - largest >= amount - 1 else 0
    counts, surplus = [largest] + [least] * (amount - 1), total - largest - least * (amount - 1)
    while surplus > 0:
        movable = [i for i in range(1, amount) if counts[i] < largest] or [i for i in range(1, amount) if counts[i] < reach]
        mass, left = sum([loads[i] for i in movable]), surplus
        for i in movable:
            extra = min(reach - counts[i], max(1, left * loads[i] // mass), surplus)
            counts[i] = counts[i] + extra
            surplus = surplus - extra
    return np.array(counts)


def scatter_about(key, dims, scale, limit, shards=(), held_as=jnp.bfloat16):
    loudness = shard_levels(key, dims, shards, -0.22, 0.18) if shards else 1.0
    entries = jax.random.normal(key, dims, jnp.float32) * scale * loudness
    return jnp.minimum(jnp.maximum(entries, -limit), limit).astype(held_as)


def setup_inputs(seed: int = 0) -> dict:
    key_of = jax.random.split(jax.random.key(seed), 14)
    tokens_in = scatter_about(key_of[0], (TOKENS, D), 1.0, 6.0, ((0, 8),))
    queries = scatter_about(key_of[1], (TOKENS, HEADS * HD), 1.0, 6.0, ((0, 8), (1, 32)))
    keys = scatter_about(key_of[2], (TOKENS, HEADS * HD), 1.0, 6.0, ((0, 8), (1, 32)))
    values = scatter_about(key_of[3], (TOKENS, HEADS * HD), 1.0, 6.0, ((0, 8), (1, 32)))
    log_decay = draw_log_decay(jax.random.fold_in(key_of[13], 71), 0)
    incoming_state = scatter_about(key_of[5], (HEADS, HD, HD), 2.0, 12.0, ((0, 32),), jnp.float32)
    attn_gain = jnp.clip(1.0 + 0.18 * jax.random.normal(key_of[6], (HEADS * HD,), jnp.float32), 0.1, 1.9)
    w_out = scatter_about(key_of[7], (HEADS * HD, D), (HEADS * HD) ** -0.5, 0.0625, ((0, 32),))
    ffn_gain = jnp.clip(1.0 + 0.18 * jax.random.normal(key_of[8], (D,), jnp.float32), 0.1, 1.9)
    router = scatter_about(key_of[9], (D, E_WIN), D ** -0.5, 0.078125)
    expert_ids_keys = jax.random.split(jax.random.fold_in(key_of[10], 1), TOKENS // TOK_DEV)
    expert_ids_turns = jax.random.permutation(jax.random.fold_in(key_of[10], 3), TOKENS // TOK_DEV)
    expert_ids = jax.vmap(lambda own, number: deal_out(jax.random.fold_in(key_of[10], 2), own, number, TOK_DEV, E_WIN, 2, CAP, 2))(expert_ids_keys, expert_ids_turns).reshape((TOKENS, 2))
    w_in = scatter_about(key_of[11], (2, E_WIN * FF, D), D ** -0.5, 0.078125, ((1, 256),))
    w_down = scatter_about(key_of[12], (E_WIN * FF, D), FF ** -0.5, 0.0625, ((0, 256),))
    return {"tokens_in": tokens_in, "queries": queries, "keys": keys, "values": values, "log_decay": log_decay, "incoming_state": incoming_state, "attn_gain": attn_gain, "w_out": w_out, "ffn_gain": ffn_gain, "router": router, "expert_ids": expert_ids, "w_in": w_in, "w_down": w_down}


HIGHEST = lax.Precision.HIGHEST
epsilon = 1e-06

def rms_scale(values_f32, gain):
    mean_square = lax.optimization_barrier(jnp.mean(values_f32 * values_f32, axis=-1, keepdims=True))
    return values_f32 * lax.rsqrt(mean_square + epsilon) * gain

def head_attention(q_rows, k_rows, v_rows, decay_row, state_start):
    scale = HD ** (-0.5)
    blocks = TOKENS // TOK_DEV
    q_blocks = q_rows.reshape(blocks, TOK_DEV, HD)
    k_blocks = k_rows.reshape(blocks, TOK_DEV, HD)
    v_blocks = v_rows.reshape(blocks, TOK_DEV, HD)
    d_blocks = decay_row.reshape(blocks, TOK_DEV)
    lower = jnp.arange(TOK_DEV)[:, None] >= jnp.arange(TOK_DEV)[None, :]

    def advance(state, block_payload):
        q_block, k_block, v_block, d_block = block_payload
        cumulative = jnp.cumsum(d_block)
        gap = jnp.where(lower, cumulative[:, None] - cumulative[None, :], 0.0)
        weight = jnp.where(lower, jnp.exp(gap), 0.0)
        scores = jnp.dot(q_block, k_block.T, preferred_element_type=jnp.float32) * scale * weight
        v_float = v_block.astype(jnp.float32)
        query_scaled = q_block.astype(jnp.float32) * (scale * jnp.exp(cumulative))[:, None]
        result = jnp.dot(scores, v_float, precision=HIGHEST) + jnp.dot(query_scaled, state, precision=HIGHEST)
        tail = jnp.exp(cumulative[-1] - cumulative)
        key_scaled = k_block.astype(jnp.float32) * tail[:, None]
        new_state = jnp.exp(cumulative[-1]) * state + jnp.dot(key_scaled.T, v_float, precision=HIGHEST)
        return (new_state, result)
    final_state, results = lax.scan(advance, state_start, (q_blocks, k_blocks, v_blocks, d_blocks))
    return results.reshape(TOKENS, HD)

def attend_pack(pack):
    return head_attention(pack[0], pack[1], pack[2], pack[3], pack[4])

def reference(tokens_in, queries, keys, values, log_decay, incoming_state, attn_gain, w_out, ffn_gain, router, expert_ids, w_in, w_down):
    q_heads = queries.reshape(TOKENS, HEADS, HD).transpose(1, 0, 2)
    k_heads = keys.reshape(TOKENS, HEADS, HD).transpose(1, 0, 2)
    v_heads = values.reshape(TOKENS, HEADS, HD).transpose(1, 0, 2)
    attended = lax.map(attend_pack, (q_heads, k_heads, v_heads, log_decay, incoming_state))
    head_normed = rms_scale(attended, attn_gain.reshape(HEADS, 1, HD)).astype(jnp.bfloat16)
    attn_heads = head_normed.transpose(1, 0, 2).reshape(TOKENS, HEADS * HD)
    attn = jnp.dot(attn_heads, w_out, preferred_element_type=jnp.float32)
    mid = tokens_in.astype(jnp.float32) + attn
    normed = rms_scale(mid, ffn_gain).astype(jnp.bfloat16)
    logits = jnp.dot(normed, router, preferred_element_type=jnp.float32)
    chosen = jnp.take_along_axis(logits, expert_ids, axis=1)
    sigmoid_gate = jax.nn.sigmoid(chosen)
    gates = sigmoid_gate / lax.optimization_barrier(jnp.sum(sigmoid_gate, axis=1, keepdims=True))
    moe = jnp.zeros((TOKENS, D), jnp.float32)
    for expert in range(E_WIN):
        gate_row_values = w_in[0, expert * FF:(expert + 1) * FF]
        up_rows = w_in[1, expert * FF:(expert + 1) * FF]
        gate_value = jnp.dot(normed, gate_row_values.T, preferred_element_type=jnp.float32)
        up_value = jnp.dot(normed, up_rows.T, preferred_element_type=jnp.float32)
        hidden = (jax.nn.silu(gate_value) * up_value).astype(jnp.bfloat16)
        down_rows = w_down[expert * FF:(expert + 1) * FF]

        def add_slice(index, total):
            start = (index * SLICE).astype(jnp.int32)
            columns = lax.dynamic_slice_in_dim(hidden, start, SLICE, 1)
            weights_part = lax.dynamic_slice_in_dim(down_rows, start, SLICE, 0)
            piece = lax.optimization_barrier(jnp.dot(columns, weights_part, preferred_element_type=jnp.float32).astype(jnp.bfloat16))
            return total + piece.astype(jnp.float32)
        expert_out = lax.fori_loop(0, FF // SLICE, add_slice, jnp.zeros((TOKENS, D), jnp.float32))
        weight_here = lax.optimization_barrier(jnp.sum(jnp.where(expert_ids == expert, gates, 0.0), axis=1))
        moe = moe + weight_here[:, None] * expert_out
    return (mid + moe).astype(jnp.bfloat16)
```

```python
import functools

import jax
import jax.numpy as jnp
from jax import lax
from jax.experimental import pallas as pl
from jax.experimental.pallas import tpu as pltpu
from jax.sharding import PartitionSpec as P

MESH = pl.DeviceIdType.MESH
HI = lax.Precision.HIGHEST
F32 = jnp.float32
BF = jnp.bfloat16
EPS = 1e-06

D = 6144
T = 128
HD = 128
CAP = 80
SL = 144
HALF = D // 2
FB = HALF // 8
OUT = D // 32

HOPS = ((4, 4, 3, 3), (3, 3, 4, 4))
HOPB = (4, 3)


def nt(a, b, precision=None):
    return lax.dot_general(
        a, b, (((1,), (1,)), ((), ())), preferred_element_type=F32, precision=precision
    )


def nn(a, b, precision=None):
    return jnp.dot(a, b, preferred_element_type=F32, precision=precision)


def iota2(shape, dim):
    return lax.broadcasted_iota(jnp.int32, shape, dim)


def kernel(
    tok_ref,
    q_ref,
    k_ref,
    v_ref,
    ld_ref,
    inc_ref,
    ag_ref,
    wo_ref,
    fg_ref,
    ro_ref,
    ids_ref,
    wi_ref,
    wd_ref,
    out_ref,
    WO, WI, WD, RO, TK, IDS,
    LS, TS, LB, TB, ST, WR,
    AH, PP, A1R, QQ, A2R, A3R, MID,
    PL, SR, LG, RX, XG, ACC, PS, PR, HID,
    YY, RBA, RBB, XRA, XRB, YS, FS, FR,
    loc, sib_s, sib_r, st_s, st_r, tt_s, tt_r,
    a1_s, a1_r, a2_s, a2_r, a3_s, a3_r, sx_s, sx_r, rx_s, rx_r,
    pr_s, pr_r, ax_s, ax_r, ar_s, ar_r, br_s, br_r, bx_s, bx_r,
    ra_s, ra_r, rr_s, rr_r, rb_s, rb_r, rx2_s, rx2_r, fn_s, fn_r,
):
    c = lax.axis_index("ctx")
    e = lax.axis_index("exp")
    x, k = c // 2, lax.rem(c, 2)
    y, z = e // 8, lax.rem(e, 8)
    b = k * 8 + z
    pend = []

    def xx(d):
        return lax.rem(x + (d + 8), 4)

    def yv(d):
        return lax.rem(y + (d + 8), 4)

    def zz(o):
        return lax.rem(z + (o + 16), 8)

    def send(src, dst, ss, rs, dc, de, keep=True):
        cp = pltpu.make_async_remote_copy(
            src_ref=src, dst_ref=dst, send_sem=ss, recv_sem=rs,
            device_id=(dc, de), device_id_type=MESH,
        )
        cp.start()
        if keep:
            pend.append(cp)
        return cp

    def arrive(dst, ss, rs):
        pltpu.make_async_remote_copy(
            src_ref=dst, dst_ref=dst, send_sem=ss, recv_sem=rs,
            device_id=(c, e), device_id_type=MESH,
        ).wait_recv()

    def cols(i, n):
        return pl.ds(pl.multiple_of(i * n, 128), n)

    bar = pltpu.get_barrier_semaphore()

    def hello(dc, de):
        pl.semaphore_signal(bar, inc=1, device_id=(dc, de), device_id_type=MESH)

    sibling = 2 * x + (1 - k)
    for d in range(1, 8):
        hello(lax.rem(c + d, 8), e)
    for d in range(1, 4):
        hello(c, yv(d) * 8 + z)
    for o in range(1, 8):
        hello(c, y * 8 + zz(o))
        hello(sibling, y * 8 + zz(o))
    src_b = e // 2
    src_k, src_z = src_b // 8, lax.rem(src_b, 8)
    src_mine = (src_k == k) & (src_z == z)
    for yy in range(4):
        @pl.when(jnp.logical_not(src_mine & (y == yy)))
        def _(yy=yy):
            hello(2 * x + src_k, yy * 8 + src_z)
    lc_wo = pltpu.make_async_copy(wo_ref, WO, loc.at[0])
    lc_wo.start()
    lc_tk = pltpu.make_async_copy(tok_ref.at[:, cols(b, FB)], TK.at[k], loc.at[1])
    lc_tk.start()
    lc_ro = pltpu.make_async_copy(
        ro_ref.at[pl.ds(pl.multiple_of(b * FB, 16), FB)], RO, loc.at[2]
    )
    lc_ro.start()

    row_i = iota2((T, T), 0)
    col_i = iota2((T, T), 1)
    lower = row_i >= col_i
    scale = HD ** (-0.5)
    cums = []
    for h in range(2):
        hs = slice(h * HD, (h + 1) * HD)
        ld = ld_ref[h:h + 1, :]
        cum = jnp.sum(jnp.where(lower, ld, 0.0), axis=1, keepdims=True)
        tot = jnp.sum(ld, axis=1, keepdims=True)
        cums.append(cum)
        ks = k_ref[:, hs].astype(F32) * jnp.exp(tot - cum)
        LS[h] = nn(ks.T, v_ref[:, hs].astype(F32), HI).astype(BF)
        TS[h:h + 1, :] = jnp.broadcast_to(tot, (1, T))
    TS[2:, :] = jnp.zeros((6, T), F32)
    idc = ids_ref[...].astype(F32)
    ident = row_i == col_i
    r0 = jnp.sum(jnp.where(ident, idc[:, 0:1], 0.0), axis=0, keepdims=True)
    r1 = jnp.sum(jnp.where(ident, idc[:, 1:2], 0.0), axis=0, keepdims=True)
    sub8 = iota2((8, T), 0)
    IDS[k] = jnp.where(sub8 == 0, r0, jnp.where(sub8 == 1, r1, 0.0))

    pl.semaphore_wait(bar, 28 - (src_mine).astype(jnp.int32))

    for d in range(1, 8):
        @pl.when(c + d < 8)
        def _(d=d):
            send(TS, TB.at[d - 1], tt_s.at[d - 1], tt_r.at[d - 1], c + d, e, False)
            send(LS, LB.at[d - 1], st_s.at[d - 1], st_r.at[d - 1], c + d, e, False)

    ob = (1 - k) * 8 + z
    send(tok_ref.at[:, cols(ob, FB)], TK.at[k], sib_s.at[0], sib_r.at[0], sibling, e)
    send(IDS.at[k], IDS.at[k], sib_s.at[1], sib_r.at[1], sibling, e)
    mine, other = cols(k, HALF), cols(1 - k, HALF)
    lc_wi = pltpu.make_async_copy(wi_ref.at[:, :, mine], WI.at[k], loc.at[3])
    lc_wi.start()
    lc_wd = pltpu.make_async_copy(wd_ref.at[:, mine], WD.at[k], loc.at[4])
    lc_wd.start()
    send(wi_ref.at[:, :, other], WI.at[k], sib_s.at[2], sib_r.at[2], sibling, e)
    send(wd_ref.at[:, other], WD.at[k], sib_s.at[3], sib_r.at[3], sibling, e)

    intra, qsc = [], []
    for h in range(2):
        hs = slice(h * HD, (h + 1) * HD)
        cum = cums[h]
        cb = jnp.broadcast_to(cum, (T, T))
        gap = jnp.where(lower, cb - cb.T, 0.0)
        weight = jnp.where(lower, jnp.exp(gap), 0.0)
        sc = nt(q_ref[:, hs], k_ref[:, hs]) * scale * weight
        intra.append(nn(sc, v_ref[:, hs].astype(F32), HI))
        qsc.append(q_ref[:, hs].astype(F32) * (scale * jnp.exp(cum)))

    ST[...] = jnp.zeros_like(ST)
    WR[...] = jnp.zeros_like(WR)
    for d in range(1, 8):
        @pl.when(c >= d)
        def _(d=d):
            arrive(TB.at[d - 1], tt_s.at[d - 1], tt_r.at[d - 1])
            arrive(LB.at[d - 1], st_s.at[d - 1], st_r.at[d - 1])
            for h in range(2):
                ST[h] = ST[h] + jnp.exp(WR[h:h + 1, :]) * LB[d - 1, h].astype(F32)
            WR[...] = WR[...] + TB[d - 1]
    for h in range(2):
        hs = slice(h * HD, (h + 1) * HD)
        state = ST[h] + jnp.exp(WR[h:h + 1, :]) * inc_ref[h]
        att = intra[h] + nn(qsc[h], state, HI)
        ms = jnp.mean(att * att, axis=1, keepdims=True)
        AH[:, hs] = (att * lax.rsqrt(ms + EPS) * ag_ref[h:h + 1, :]).astype(BF)

    lc_wo.wait()
    for kc in range(2):
        def project(i, carry, kc=kc):
            cs = pl.ds(pl.multiple_of(kc * HALF + i * 512, 128), 512)
            PP[:, cs] = nn(AH[...], WO[:, cs]).astype(BF)
            return carry
        lax.fori_loop(0, HALF // 512, project, 0)
        for d in (2, 1, 3):
            i = kc * 3 + d - 1
            cs = slice(kc * HALF, (kc + 1) * HALF)
            send(
                PP.at[pl.ds(pl.multiple_of(yv(d) * 32, 32), 32), cs],
                A1R.at[d - 1, :, cs],
                a1_s.at[i], a1_r.at[i], c, yv(d) * 8 + z,
            )
    for kc in range(2):
        cs = slice(kc * HALF, (kc + 1) * HALF)
        for d in range(1, 4):
            i = kc * 3 + d - 1
            arrive(A1R.at[d - 1, :, cs], a1_s.at[i], a1_r.at[i])

        def add_y(i, carry, kc=kc):
            s = pl.ds(pl.multiple_of(kc * HALF + i * 512, 128), 512)
            acc = PP[pl.ds(pl.multiple_of(y * 32, 32), 32), s].astype(F32)
            for d in range(3):
                acc = acc + A1R[d, :, s].astype(F32)
            QQ[:, s] = acc.astype(BF)
            return carry
        lax.fori_loop(0, HALF // 512, add_y, 0)
        dest = 2 * x + kc
        for o in (4, 3, 5, 2, 6, 1, 7):
            send(
                QQ.at[:, cols(kc * 8 + zz(o), FB)],
                A2R.at[k, o], a2_s.at[kc, o], a2_r.at[k, o], dest, y * 8 + zz(o),
            )
        own = cols(kc * 8 + z, FB)

        @pl.when(k == kc)
        def _(own=own):
            A2R[k, 0] = QQ[:, own]

        @pl.when(k != kc)
        def _(own=own, kc=kc, dest=dest):
            send(QQ.at[:, own], A2R.at[k, 0], a2_s.at[kc, 0], a2_r.at[k, 0], dest, e, False)

    for kc in range(2):
        @pl.when(k != kc)
        def _(kc=kc):
            arrive(A2R.at[kc, 0], a2_s.at[kc, 0], a2_r.at[kc, 0])
        acc = A2R[kc, 0].astype(F32)
        for o in range(1, 8):
            arrive(A2R.at[kc, o], a2_s.at[kc, o], a2_r.at[kc, o])
            acc = acc + A2R[kc, o].astype(F32)
        A3R[0, kc] = acc.astype(BF)
    for d in range(1, 4):
        send(A3R.at[0], A3R.at[d], a3_s.at[d - 1], a3_r.at[d - 1], c, yv(d) * 8 + z)

    arrive(IDS.at[1 - k], sib_s.at[1], sib_r.at[1])
    strict = (row_i < col_i).astype(BF)
    yf = y.astype(F32)
    for kc in range(2):
        mask = ((IDS[kc, 0:1, :] == yf) | (IDS[kc, 1:2, :] == yf)).astype(F32)
        before = nn(jnp.broadcast_to(mask, (8, T)).astype(BF), strict)[0:1, :]
        PL[kc] = jnp.where(
            (row_i.astype(F32) == before) & (row_i < CAP), mask, 0.0
        )

    lc_tk.wait()
    arrive(TK.at[1 - k], sib_s.at[0], sib_r.at[0])
    lc_ro.wait()
    gain = jnp.concatenate([fg_ref[pl.ds(b * 3 + i, 1), :] for i in range(3)], axis=1)
    for d in range(4):
        if d:
            arrive(A3R.at[d], a3_s.at[d - 1], a3_r.at[d - 1])
        rows = pl.ds(pl.multiple_of(yv(-d) * 32, 32), 32)
        for kc in range(2):
            MID[kc, rows, :] = TK[kc, rows, :].astype(F32) + A3R[d, kc].astype(F32)

    def rows_a(i):
        return pl.ds(pl.multiple_of(i * 160, 16), 80)

    def rows_b(i):
        return pl.ds(pl.multiple_of(i * 160 + 80, 16), 80)

    def piece_a(zs, d):
        return XG.at[zs, rows_a(xx(-d))]

    def piece_b(zs, d):
        return XG.at[zs, rows_b(xx(-d))]

    step_dir = (1, -1)

    def alpha_ring(r, d, h):
        p = piece_a(zz(-step_dir[r] * (h - 1)), d)
        send(p, p, ar_s.at[r, d, h - 1], ar_r.at[r, d, h - 1], c, y * 8 + zz(step_dir[r]))

    def beta_ring(r, h):
        p = piece_b(zz(-step_dir[r] * (h - 1)), 0)
        send(p, p, br_s.at[r, h - 1], br_r.at[r, h - 1], c, y * 8 + zz(step_dir[r]))

    def beta_x(o):
        p = piece_b(zz(o), 0)
        for d in range(1, 4):
            send(p, p, bx_s.at[o % 8, d - 1], bx_r.at[o % 8, d - 1], 2 * xx(d) + k, e)

    def beta_x_wait(o):
        for d in range(1, 4):
            arrive(piece_b(zz(o), d), bx_s.at[o % 8, d - 1], bx_r.at[o % 8, d - 1])

    for kc in (1, 0):
        xg = (MID[kc] * gain).astype(BF)
        slots = nn(PL[kc, :CAP, :].astype(BF), xg).astype(BF)
        if kc:
            XG[z, rows_b(x), :] = slots
            beta_ring(0, 1)
            beta_ring(1, 1)
        else:
            XG[z, rows_a(x), :] = slots
            pa = piece_a(z, 0)
            for d in range(1, 4):
                send(pa, pa, ax_s.at[d - 1], ax_r.at[d - 1], 2 * xx(d) + k, e)
            alpha_ring(0, 0, 1)
            alpha_ring(1, 0, 1)
            beta_x(0)
    lane = iota2((T, T), 1)
    for kc in range(2):
        m = MID[kc]
        lg = nn((m * gain).astype(BF), RO[...])
        st = jnp.where(lane == 4, jnp.sum(m * m, axis=1, keepdims=True), 0.0)
        for j in range(4):
            st = jnp.where(lane == j, lg[:, j:j + 1], st)
        SR[0, :, kc * T:(kc + 1) * T] = st.T[0:8, :]
    for o in range(16):
        if o:
            dk = o // 8
            send(
                SR.at[0], SR.at[o], sx_s.at[o], sx_r.at[o],
                sibling if dk else c, y * 8 + zz(o % 8),
            )

    lc_wi.wait()
    arrive(WI.at[1 - k], sib_s.at[2], sib_r.at[2])

    def ffn_in(o, first=False):
        zs = zz(o)
        ws = cols(zs, FB)

        def body(i, carry):
            rows = pl.ds(pl.multiple_of(i * 160, 16), 160)
            xb = XG[zs, rows, :]
            for q in range(4):
                r = nt(xb, WI[q // 2, q % 2, :, ws])
                if first:
                    ACC[q, rows, :] = r
                else:
                    ACC[q, rows, :] = ACC[q, rows, :] + r
            return carry
        lax.fori_loop(0, 4, body, 0)

    for h in range(1, 5):
        for r in range(2):
            if h <= HOPB[r]:
                arrive(piece_b(zz(-step_dir[r] * h), 0), br_s.at[r, h - 1], br_r.at[r, h - 1])
                if h < HOPB[r]:
                    beta_ring(r, h + 1)
                beta_x(-step_dir[r] * h)
        for d in range(4):
            if h == 1 and d:
                arrive(piece_a(z, d), ax_s.at[d - 1], ax_r.at[d - 1])
                alpha_ring(0, d, 1)
                alpha_ring(1, d, 1)
        for d in range(4):
            for r in range(2):
                if h <= HOPS[r][d]:
                    arrive(
                        piece_a(zz(-step_dir[r] * h), d),
                        ar_s.at[r, d, h - 1], ar_r.at[r, d, h - 1],
                    )
                    if h < HOPS[r][d]:
                        alpha_ring(r, d, h + 1)
        if h == 1:
            beta_x_wait(0)
            ffn_in(0, True)
            for o in range(1, 16):
                arrive(SR.at[o], sx_s.at[o], sx_r.at[o])
            tot = SR[0]
            for o in range(1, 16):
                tot = tot + SR[o]
            rstd = lax.rsqrt(tot[4:5, :] / D + EPS)
            LG[...] = tot * rstd
            rs = jnp.concatenate(
                [
                    nt(jnp.broadcast_to(rstd[:, kc * T:(kc + 1) * T], (8, T)), PL[kc], HI)
                    for kc in range(2)
                ],
                axis=1,
            )
            RX[0] = rs
            for d in range(1, 4):
                send(RX.at[0], RX.at[d], rx_s.at[d - 1], rx_r.at[d - 1], 2 * xx(d) + k, e)
        else:
            for o in (h - 1, 1 - h):
                beta_x_wait(o)
                ffn_in(o)
    beta_x_wait(-4)
    ffn_in(-4)

    for g in range(2):
        PS[g] = ACC[2 * (1 - k) + g].astype(BF)
    send(PS, PR, pr_s.at[0], pr_r.at[0], sibling, e)
    for d in range(1, 4):
        arrive(RX.at[d], rx_s.at[d - 1], rx_r.at[d - 1])
    lc_wd.wait()
    arrive(WD.at[1 - k], sib_s.at[3], sib_r.at[3])
    arrive(PR, pr_s.at[0], pr_r.at[0])
    for d in range(4):
        for kc in range(2):
            rs = RX[d, 0:1, kc * T:(kc + 1) * T]
            col = jnp.broadcast_to(rs, (T, T)).T[:CAP, 0:1]
            rows = (rows_b if kc else rows_a)(xx(-d))
            g = (ACC[2 * k, rows, :] + PR[0, rows, :].astype(F32)) * col
            u = (ACC[2 * k + 1, rows, :] + PR[1, rows, :].astype(F32)) * col
            HID[k, rows, :] = (g / (1.0 + jnp.exp(-g)) * u).astype(BF)
    send(HID.at[k], HID.at[k], pr_s.at[1], pr_r.at[1], sibling, e)
    arrive(HID.at[1 - k], pr_s.at[1], pr_r.at[1])

    def down(o):
        zs = zz(o)
        ws = cols(zs, FB)

        def body(i, carry):
            rows = pl.ds(pl.multiple_of(i * 160, 16), 160)
            r = nn(HID[0, rows, :], WD[0, :, ws]) + nn(HID[1, rows, :], WD[1, :, ws])
            YY[zs, rows, :] = r.astype(BF)
            return carry
        lax.fori_loop(0, 4, body, 0)

    def back_ring(r, d, s):
        hops = HOPS[r][d]
        zs = zz(step_dir[r] * (hops - s))
        p = YY.at[zs, rows_a(xx(d))]
        if s:
            arrive(RBA.at[r, d, s - 1], rr_s.at[r, d, s - 1], rr_r.at[r, d, s - 1])
            p[...] = (p[...].astype(F32) + RBA[r, d, s - 1].astype(F32)).astype(BF)
        send(p, RBA.at[r, d, s], rr_s.at[r, d, s], rr_r.at[r, d, s], c, y * 8 + zz(step_dir[r]))

    def back_x(o):
        for d in range(1, 4):
            send(
                YY.at[zz(o), rows_b(xx(d))], XRB.at[o % 8, d - 1],
                rx2_s.at[o % 8, d - 1], rx2_r.at[o % 8, d - 1], 2 * xx(d) + k, e,
            )

    def back_x_sum(o):
        acc = YY[zz(o), rows_b(x), :].astype(F32)
        for d in range(1, 4):
            arrive(XRB.at[o % 8, d - 1], rx2_s.at[o % 8, d - 1], rx2_r.at[o % 8, d - 1])
            acc = acc + XRB[o % 8, d - 1].astype(F32)
        return acc

    def back_ring_b(r, s):
        o = step_dir[r] * (HOPB[r] - s)
        acc = back_x_sum(o)
        if s:
            arrive(RBB.at[r, s - 1], rb_s.at[r, s - 1], rb_r.at[r, s - 1])
            acc = acc + RBB[r, s - 1].astype(F32)
        p = YY.at[zz(o), rows_b(x)]
        p[...] = acc.astype(BF)
        send(p, RBB.at[r, s], rb_s.at[r, s], rb_r.at[r, s], c, y * 8 + zz(step_dir[r]))

    for o in (4, 3, -3, -2, 2, -1, 1, 0):
        down(o)
        for r in range(2):
            for d in range(4):
                if (step_dir[r] * HOPS[r][d] - o) % 8 == 0:
                    back_ring(r, d, 0)
        back_x(o)
    for s in range(1, 5):
        for d in range(4):
            for r in range(2):
                if s < HOPS[r][d]:
                    back_ring(r, d, s)
        for r in range(2):
            if s - 1 < HOPB[r]:
                back_ring_b(r, s - 1)
    for d in (2, 1, 3, 0):
        acc = YY[z, rows_a(xx(d)), :].astype(F32)
        for r in range(2):
            s = HOPS[r][d] - 1
            arrive(RBA.at[r, d, s], rr_s.at[r, d, s], rr_r.at[r, d, s])
            acc = acc + RBA[r, d, s].astype(F32)
        if d:
            p = YY.at[z, rows_a(xx(d))]
            p[...] = acc.astype(BF)
            send(p, XRA.at[d - 1], ra_s.at[d - 1], ra_r.at[d - 1], 2 * xx(d) + k, e)
        else:
            YS[0, :CAP, :] = acc
    acc = back_x_sum(0)
    for r in range(2):
        s = HOPB[r] - 1
        arrive(RBB.at[r, s], rb_s.at[r, s], rb_r.at[r, s])
        acc = acc + RBB[r, s].astype(F32)
    YS[1, :CAP, :] = acc
    acc = YS[0, :CAP, :]
    for d in range(1, 4):
        arrive(XRA.at[d - 1], ra_s.at[d - 1], ra_r.at[d - 1])
        acc = acc + XRA[d - 1].astype(F32)
    YS[0, :CAP, :] = acc

    first = (y == 0).astype(F32)
    target = 2 * b
    to_me = (target == e) | (target + 1 == e)
    for kc in range(2):
        sg = 1.0 / (1.0 + jnp.exp(-LG[:, kc * T:(kc + 1) * T]))
        i0, i1 = IDS[kc, 0:1, :], IDS[kc, 1:2, :]
        den = jnp.zeros((1, T), F32)
        num = jnp.zeros((1, T), F32)
        for j in range(4):
            hit = ((i0 == j) | (i1 == j)).astype(F32) * sg[j:j + 1, :]
            den = den + hit
            num = num + jnp.where(y == j, hit, 0.0)
        gate = num / den
        got = nn((PL[kc] * gate).T[:, :CAP], YS[kc, :CAP, :], HI)
        got = got + first * MID[kc]
        for j in range(2):
            FS[kc * 2 + j] = got[:, j * OUT:(j + 1) * OUT].astype(BF)
            dc, de = 2 * x + kc, target + j
            is_me = (k == kc) & (de == e)

            @pl.when(is_me)
            def _(i=kc * 2 + j):
                FR[y] = FS[i]

            @pl.when(jnp.logical_not(is_me))
            def _(i=kc * 2 + j, dc=dc, de=de):
                send(FS.at[i], FR.at[y], fn_s.at[i], fn_r.at[y], dc, de, False)

    for yy in range(4):
        @pl.when(jnp.logical_not(src_mine & (y == yy)))
        def _(yy=yy):
            arrive(FR.at[yy], fn_s.at[yy], fn_r.at[yy])
    acc = FR[0].astype(F32)
    for yy in range(1, 4):
        acc = acc + FR[yy].astype(F32)
    out_ref[...] = acc.astype(BF)

    def left(src, ss):
        pltpu.make_async_remote_copy(
            src_ref=src, dst_ref=src, send_sem=ss, recv_sem=ss,
            device_id=(c, e), device_id_type=MESH,
        ).wait_send()

    for cp in pend:
        cp.wait_send()
    for d in range(1, 8):
        @pl.when(c + d < 8)
        def _(d=d):
            left(TS, tt_s.at[d - 1])
            left(LS, st_s.at[d - 1])
    for kc in range(2):
        @pl.when(k != kc)
        def _(kc=kc):
            left(QQ.at[:, cols(kc * 8 + z, FB)], a2_s.at[kc, 0])
        for j in range(2):
            @pl.when(jnp.logical_not((k == kc) & (target + j == e)))
            def _(i=kc * 2 + j):
                left(FS.at[i], fn_s.at[i])


def local(tok, q, kk, v, ld, inc, ag, wo, fg, ro, ids, wi, wd):
    vm = lambda *s, t=BF: pltpu.VMEM(s, t)
    dma = lambda *s: pltpu.SemaphoreType.DMA(s)
    inside = pl.BlockSpec(memory_space=pltpu.VMEM)
    outside = pl.BlockSpec(memory_space=pl.ANY)
    scratch = [
        vm(256, D), vm(2, 2, SL, HALF), vm(2, SL, HALF), vm(FB, 4), vm(2, T, FB), vm(2, 8, T, t=F32),
        vm(2, HD, HD), vm(8, T, t=F32), vm(7, 2, HD, HD), vm(7, 8, T, t=F32),
        vm(2, HD, HD, t=F32), vm(8, T, t=F32),
        vm(T, 2 * HD), vm(T, D), vm(3, 32, D), vm(32, D), vm(2, 8, 32, FB), vm(4, 2, 32, FB),
        vm(2, T, FB, t=F32),
        vm(2, T, T, t=F32), vm(16, 8, 2 * T, t=F32), vm(8, 2 * T, t=F32), vm(4, 8, 2 * T, t=F32), vm(8, 8 * CAP, FB),
        vm(4, 8 * CAP, SL, t=F32), vm(2, 8 * CAP, SL), vm(2, 8 * CAP, SL), vm(2, 8 * CAP, SL),
        vm(8, 8 * CAP, FB), vm(2, 4, 4, CAP, FB), vm(2, 4, CAP, FB), vm(3, CAP, FB), vm(8, 3, CAP, FB),
        vm(2, CAP, FB, t=F32), vm(4, T, OUT), vm(4, T, OUT),
        dma(5), dma(4), dma(4), dma(7), dma(7), dma(7), dma(7),
        dma(6), dma(6), dma(2, 8), dma(2, 8), dma(3), dma(3), dma(16), dma(16), dma(3), dma(3),
        dma(2), dma(2), dma(3), dma(3), dma(2, 4, 4), dma(2, 4, 4), dma(2, 4), dma(2, 4), dma(8, 3), dma(8, 3),
        dma(3), dma(3), dma(2, 4, 4), dma(2, 4, 4), dma(2, 4), dma(2, 4), dma(8, 3), dma(8, 3), dma(4), dma(4),
    ]
    return pl.pallas_call(
        kernel,
        out_shape=jax.ShapeDtypeStruct((T, OUT), BF),
        in_specs=[
            outside, inside, inside, inside, inside, inside, inside,
            outside, inside, outside, inside, outside, outside,
        ],
        out_specs=inside,
        scratch_shapes=scratch,
        compiler_params=pltpu.CompilerParams(
            collective_id=0, has_side_effects=True, vmem_limit_bytes=56 * 2**20
        ),
        cost_estimate=pl.CostEstimate(flops=4 * 10**9, bytes_accessed=10**7, transcendentals=10**5),
    )(tok, q, kk, v, ld, inc, ag.reshape(2, HD), wo, fg.reshape(D // 128, 128), ro, ids, wi, wd)


def solution(mesh):
    return jax.shard_map(
        local,
        mesh=mesh,
        in_specs=(
            P("ctx", None),
            P("ctx", "exp"),
            P("ctx", "exp"),
            P("ctx", "exp"),
            P("exp", "ctx"),
            P("exp", None, None),
            P("exp"),
            P("exp", None),
            P(),
            P(),
            P("ctx", None),
            P(None, ("exp", "ctx"), None),
            P(("exp", "ctx"), None),
        ),
        out_specs=P("ctx", "exp"),
        check_vma=False,
    )
```

```python
import functools

import jax
import jax.numpy as jnp
from jax import lax
from jax.experimental import pallas as pl
from jax.experimental.pallas import tpu as pltpu
from jax.sharding import PartitionSpec as P

MESH = pl.DeviceIdType.MESH
HI = lax.Precision.HIGHEST
F32 = jnp.float32
BF = jnp.bfloat16
EPS = 1e-06

D = 6144
T = 128
HD = 128
CAP = 80
SL = 144
HALF = D // 2
FB = HALF // 8
OUT = D // 32
FZ = 128
FY = FB - FZ
DY = 16 * FY

HOPS = ((4, 4, 3, 3), (3, 3, 4, 4))
HOPB = (4, 3)


def nt(a, b, precision=None):
    return lax.dot_general(
        a, b, (((1,), (1,)), ((), ())), preferred_element_type=F32, precision=precision
    )


def nn(a, b, precision=None):
    return jnp.dot(a, b, preferred_element_type=F32, precision=precision)


def iota2(shape, dim):
    return lax.broadcasted_iota(jnp.int32, shape, dim)


def kernel(
    tok_ref,
    q_ref,
    k_ref,
    v_ref,
    ld_ref,
    inc_ref,
    ag_ref,
    wo_ref,
    fg_ref,
    ro_ref,
    ids_ref,
    wi_ref,
    wd_ref,
    out_ref,
    WO, WI, WD, TK, IDS,
    LF, LS, TS, LB, TB, ST, SO, LC, TC, IN, QS, WR,
    AH, PP, PZ, A1R, QQ, A2R, Z1R, ZQ, Z2R, A3R, MID,
    PL, PT, GC, SR, LG, RX, XG, ACC, PS, PR, HID,
    YY, RBA, RBB, XRA, XRB, YS, FS, FR,
    loc, sib_s, sib_r, st_s, st_r, tt_s, tt_r,
    a1_s, a1_r, z1_s, z1_r, z2_s, z2_r, a2_s, a2_r, a3_s, a3_r, sx_s, sx_r, rx_s, rx_r,
    pr_s, pr_r, ax_s, ax_r, ar_s, ar_r, br_s, br_r, bx_s, bx_r,
    ra_s, ra_r, rr_s, rr_r, rb_s, rb_r, rx2_s, rx2_r, fn_s, fn_r,
):
    c = lax.axis_index("ctx")
    e = lax.axis_index("exp")
    x, k = c // 2, lax.rem(c, 2)
    y, z = e // 8, lax.rem(e, 8)

    def pos(zs):
        return lax.rem(zs, 2) * 4 + zs // 2

    b = k * 8 + pos(z)
    pend = []

    def xx(d):
        return lax.rem(x + (d + 8), 4)

    def yv(d):
        return lax.rem(y + (d + 8), 4)

    def zz(o):
        return lax.rem(z + (o + 16), 8)

    def send(src, dst, ss, rs, dc, de, keep=True):
        cp = pltpu.make_async_remote_copy(
            src_ref=src, dst_ref=dst, send_sem=ss, recv_sem=rs,
            device_id=(dc, de), device_id_type=MESH,
        )
        cp.start()
        if keep:
            pend.append(cp)
        return cp

    def arrive(dst, ss, rs):
        pltpu.make_async_remote_copy(
            src_ref=dst, dst_ref=dst, send_sem=ss, recv_sem=rs,
            device_id=(c, e), device_id_type=MESH,
        ).wait_recv()

    def cols(i, n):
        return pl.ds(pl.multiple_of(i * n, 128), n)

    bar = pltpu.get_barrier_semaphore()

    def hello(dc, de):
        pl.semaphore_signal(bar, inc=1, device_id=(dc, de), device_id_type=MESH)

    sibling = 2 * x + (1 - k)
    for d in range(1, 8):
        hello(lax.rem(c + d, 8), e)
    for d in range(1, 4):
        hello(c, yv(d) * 8 + z)
    for o in range(1, 8):
        hello(c, y * 8 + zz(o))
        hello(sibling, y * 8 + zz(o))
    src_b = e // 2
    src_k, src_p = src_b // 8, lax.rem(src_b, 8)
    src_z = 2 * lax.rem(src_p, 4) + src_p // 4
    src_mine = (src_k == k) & (src_z == z)
    for yy in range(4):
        @pl.when(jnp.logical_not(src_mine & (y == yy)))
        def _(yy=yy):
            hello(2 * x + src_k, yy * 8 + src_z)
    lc_wo = pltpu.make_async_copy(wo_ref, WO, loc.at[0])
    lc_wo.start()
    lc_tk = pltpu.make_async_copy(tok_ref.at[:, cols(b, FB)], TK.at[k], loc.at[1])
    lc_tk.start()

    row_i = iota2((T, T), 0)
    col_i = iota2((T, T), 1)
    lower = row_i >= col_i
    scale = HD ** (-0.5)
    cums = []
    for h in range(2):
        hs = slice(h * HD, (h + 1) * HD)
        ld = ld_ref[h:h + 1, :]
        cum = jnp.sum(jnp.where(lower, ld, 0.0), axis=1, keepdims=True)
        tot = jnp.sum(ld, axis=1, keepdims=True)
        cums.append(cum)
        ks = k_ref[:, hs].astype(F32) * jnp.exp(tot - cum)
        LF[h] = nn(ks.T, v_ref[:, hs].astype(F32), HI)
        LS[h] = LF[h].astype(BF)
        TS[h:h + 1, :] = jnp.broadcast_to(tot, (1, T))
    TS[2:, :] = jnp.zeros((6, T), F32)
    IDS[k, 0:2, :] = ids_ref[...].astype(F32)
    IDS[k, 2:8, :] = jnp.zeros((6, T), F32)

    pl.semaphore_wait(bar, 28 - (src_mine).astype(jnp.int32))

    send(TS, TB.at[0], tt_s.at[0], tt_r.at[0], sibling, e)
    send(LS.at[1 - k], LB.at[0], st_s.at[0], st_r.at[0], sibling, e)
    ob = (1 - k) * 8 + pos(z)
    send(tok_ref.at[:, cols(ob, FB)], TK.at[k], sib_s.at[0], sib_r.at[0], sibling, e)
    send(IDS.at[k], IDS.at[k], sib_s.at[1], sib_r.at[1], sibling, e)
    mine, other = cols(k, HALF), cols(1 - k, HALF)
    lc_wi = pltpu.make_async_copy(wi_ref.at[:, :, mine], WI.at[k], loc.at[3])
    lc_wi.start()
    lc_wd = pltpu.make_async_copy(wd_ref.at[:, mine], WD.at[k], loc.at[4])
    lc_wd.start()
    send(wi_ref.at[:, :, other], WI.at[k], sib_s.at[2], sib_r.at[2], sibling, e)
    send(wd_ref.at[:, other], WD.at[k], sib_s.at[3], sib_r.at[3], sibling, e)

    arrive(TB.at[0], tt_s.at[0], tt_r.at[0])
    arrive(LB.at[0], st_s.at[0], st_r.at[0])
    mine_l, other_l = LF[k], LB[0].astype(F32)
    mine_t, other_t = TS[pl.ds(k, 1), :], TB[0, pl.ds(k, 1), :]
    core0 = k == 0
    l0 = jnp.where(core0, mine_l, other_l)
    l1 = jnp.where(core0, other_l, mine_l)
    t0 = jnp.where(core0, mine_t, other_t)
    t1 = jnp.where(core0, other_t, mine_t)
    LC[...] = (jnp.exp(t1) * l0 + l1).astype(BF)
    TC[...] = jnp.broadcast_to(t0 + t1, (8, T))
    for d in range(1, 4):
        @pl.when(x + d < 4)
        def _(d=d):
            send(TC, TB.at[d], tt_s.at[d], tt_r.at[d], c + 2 * d, e, False)
            send(LC, LB.at[d], st_s.at[d], st_r.at[d], c + 2 * d, e, False)

    for h in range(2):
        hs = slice(h * HD, (h + 1) * HD)
        cum = cums[h]
        cb = jnp.broadcast_to(cum, (T, T))
        gap = jnp.where(lower, cb - cb.T, 0.0)
        weight = jnp.where(lower, jnp.exp(gap), 0.0)
        sc = nt(q_ref[:, hs], k_ref[:, hs]) * scale * weight
        IN[h] = nn(sc, v_ref[:, hs].astype(F32), HI)
        QS[h] = q_ref[:, hs].astype(F32) * (scale * jnp.exp(cum))

    ST[k] = jnp.zeros((HD, HD), F32)
    WR[...] = jnp.zeros_like(WR)
    for d in range(1, 4):
        @pl.when(x >= d)
        def _(d=d):
            arrive(TB.at[d], tt_s.at[d], tt_r.at[d])
            arrive(LB.at[d], st_s.at[d], st_r.at[d])
            ST[k] = ST[k] + jnp.exp(WR[0:1, :]) * LB[d].astype(F32)
            WR[...] = WR[...] + TB[d]
    start = ST[k] + jnp.exp(WR[0:1, :]) * inc_ref[k]
    after = jnp.exp(t0) * start + l0
    ST[k] = jnp.where(core0, start, after)
    SO[...] = jnp.where(core0, after, start)
    send(SO, ST.at[k], tt_s.at[4], tt_r.at[4], sibling, e)

    def finish(h):
        att = IN[h] + nn(QS[h], ST[h], HI)
        ms = jnp.mean(att * att, axis=1, keepdims=True)
        AH[:, pl.ds(pl.multiple_of(h * HD, HD), HD)] = (
            att * lax.rsqrt(ms + EPS) * ag_ref[pl.ds(h, 1), :]
        ).astype(BF)

    finish(k)
    arrive(ST.at[1 - k], tt_s.at[4], tt_r.at[4])
    finish(1 - k)

    lc_wo.wait()
    for kc in range(2):
        def project(i, carry, kc=kc):
            bl = kc * 8 + i
            r = nn(AH[...], WO[:, cols(bl, FB)]).astype(BF)
            PP[:, cols(bl, FY)] = r[:, :FY]
            PZ[:, cols(bl, FZ)] = r[:, FY:]
            return carry
        lax.fori_loop(0, 8, project, 0)
        cs = slice(kc * 8 * FY, (kc + 1) * 8 * FY)
        for d in (2, 1, 3):
            i = kc * 3 + d - 1
            send(
                PP.at[pl.ds(pl.multiple_of(yv(d) * 32, 32), 32), cs],
                A1R.at[d - 1, :, cs],
                a1_s.at[i], a1_r.at[i], c, yv(d) * 8 + z,
            )
        dest = 2 * x + kc
        for o in (4, 3, 5, 2, 6, 1, 7):
            send(
                PZ.at[:, cols(kc * 8 + pos(zz(o)), FZ)],
                Z1R.at[k, o], z1_s.at[kc, o], z1_r.at[k, o], dest, y * 8 + zz(o),
            )
        own = cols(kc * 8 + pos(z), FZ)

        @pl.when(k == kc)
        def _(own=own):
            Z1R[k, 0] = PZ[:, own]

        @pl.when(k != kc)
        def _(own=own, kc=kc, dest=dest):
            send(PZ.at[:, own], Z1R.at[k, 0], z1_s.at[kc, 0], z1_r.at[k, 0], dest, e, False)
    for kc in range(2):
        cs = slice(kc * 8 * FY, (kc + 1) * 8 * FY)
        for d in range(1, 4):
            i = kc * 3 + d - 1
            arrive(A1R.at[d - 1, :, cs], a1_s.at[i], a1_r.at[i])

        def add_y(i, carry, kc=kc):
            s = pl.ds(pl.multiple_of(kc * 8 * FY + i * 512, 128), 512)
            acc = PP[pl.ds(pl.multiple_of(y * 32, 32), 32), s].astype(F32)
            for d in range(3):
                acc = acc + A1R[d, :, s].astype(F32)
            QQ[:, s] = acc.astype(BF)
            return carry
        lax.fori_loop(0, 8 * FY // 512, add_y, 0)
        dest = 2 * x + kc
        for o in (4, 3, 5, 2, 6, 1, 7):
            send(
                QQ.at[:, cols(kc * 8 + pos(zz(o)), FY)],
                A2R.at[k, o], a2_s.at[kc, o], a2_r.at[k, o], dest, y * 8 + zz(o),
            )
        own = cols(kc * 8 + pos(z), FY)

        @pl.when(k == kc)
        def _(own=own):
            A2R[k, 0] = QQ[:, own]

        @pl.when(k != kc)
        def _(own=own, kc=kc, dest=dest):
            send(QQ.at[:, own], A2R.at[k, 0], a2_s.at[kc, 0], a2_r.at[k, 0], dest, e, False)

    for kc in range(2):
        @pl.when(k != kc)
        def _(kc=kc):
            arrive(Z1R.at[kc, 0], z1_s.at[kc, 0], z1_r.at[kc, 0])
        acc = Z1R[kc, 0].astype(F32)
        for o in range(1, 8):
            arrive(Z1R.at[kc, o], z1_s.at[kc, o], z1_r.at[kc, o])
            acc = acc + Z1R[kc, o].astype(F32)
        ZQ[kc] = acc.astype(BF)
    for d in (2, 1, 3):
        send(
            ZQ.at[:, pl.ds(pl.multiple_of(yv(d) * 32, 32), 32)], Z2R.at[d - 1],
            z2_s.at[d - 1], z2_r.at[d - 1], c, yv(d) * 8 + z,
        )
    for kc in range(2):
        @pl.when(k != kc)
        def _(kc=kc):
            arrive(A2R.at[kc, 0], a2_s.at[kc, 0], a2_r.at[kc, 0])
        acc = A2R[kc, 0].astype(F32)
        for o in range(1, 8):
            arrive(A2R.at[kc, o], a2_s.at[kc, o], a2_r.at[kc, o])
            acc = acc + A2R[kc, o].astype(F32)
        A3R[0, kc, :, :FY] = acc.astype(BF)
    acc = ZQ[:, pl.ds(pl.multiple_of(y * 32, 32), 32), :].astype(F32)
    for d in range(1, 4):
        arrive(Z2R.at[d - 1], z2_s.at[d - 1], z2_r.at[d - 1])
        acc = acc + Z2R[d - 1].astype(F32)
    A3R[0, :, :, FY:] = acc.astype(BF)
    for d in range(1, 4):
        send(A3R.at[0], A3R.at[d], a3_s.at[d - 1], a3_r.at[d - 1], c, yv(d) * 8 + z)

    arrive(IDS.at[1 - k], sib_s.at[1], sib_r.at[1])
    strict = (row_i < col_i).astype(BF)
    yf = y.astype(F32)
    for kc in range(2):
        mask = ((IDS[kc, 0:1, :] == yf) | (IDS[kc, 1:2, :] == yf)).astype(F32)
        before = nn(jnp.broadcast_to(mask, (8, T)).astype(BF), strict)[0:1, :]
        PL[kc] = jnp.where(
            (row_i.astype(F32) == before) & (row_i < CAP), mask, 0.0
        )

    lc_tk.wait()
    arrive(TK.at[1 - k], sib_s.at[0], sib_r.at[0])
    gain = jnp.concatenate([fg_ref[pl.ds(b * 3 + i, 1), :] for i in range(3)], axis=1)
    for d in range(4):
        if d:
            arrive(A3R.at[d], a3_s.at[d - 1], a3_r.at[d - 1])
        rows = pl.ds(pl.multiple_of(yv(-d) * 32, 32), 32)
        for kc in range(2):
            MID[kc, rows, :] = TK[kc, rows, :].astype(F32) + A3R[d, kc].astype(F32)

    def rows_a(i):
        return pl.ds(pl.multiple_of(i * 160, 16), 80)

    def rows_b(i):
        return pl.ds(pl.multiple_of(i * 160 + 80, 16), 80)

    def piece_a(zs, d):
        return XG.at[zs, rows_a(xx(-d))]

    def piece_b(zs, d):
        return XG.at[zs, rows_b(xx(-d))]

    step_dir = (1, -1)

    def alpha_ring(r, d, h):
        p = piece_a(zz(-step_dir[r] * (h - 1)), d)
        send(p, p, ar_s.at[r, d, h - 1], ar_r.at[r, d, h - 1], c, y * 8 + zz(step_dir[r]))

    def beta_ring(r, h):
        p = piece_b(zz(-step_dir[r] * (h - 1)), 0)
        send(p, p, br_s.at[r, h - 1], br_r.at[r, h - 1], c, y * 8 + zz(step_dir[r]))

    def beta_x(o):
        p = piece_b(zz(o), 0)
        for d in range(1, 4):
            send(p, p, bx_s.at[o % 8, d - 1], bx_r.at[o % 8, d - 1], 2 * xx(d) + k, e)

    def beta_x_wait(o):
        for d in range(1, 4):
            arrive(piece_b(zz(o), d), bx_s.at[o % 8, d - 1], bx_r.at[o % 8, d - 1])

    for kc in (1, 0):
        xg = (MID[kc] * gain).astype(BF)
        slots = nn(PL[kc, :CAP, :].astype(BF), xg).astype(BF)
        if kc:
            XG[z, rows_b(x), :] = slots
            beta_ring(0, 1)
            beta_ring(1, 1)
        else:
            XG[z, rows_a(x), :] = slots
            pa = piece_a(z, 0)
            for d in range(1, 4):
                send(pa, pa, ax_s.at[d - 1], ax_r.at[d - 1], 2 * xx(d) + k, e)
            alpha_ring(0, 0, 1)
            alpha_ring(1, 0, 1)
            beta_x(0)
    router = ro_ref[:, cols(b, FB)]
    for kc in range(2):
        m = MID[kc]
        ts = slice(kc * T, (kc + 1) * T)
        SR[0, 0:4, ts] = nt(router, (m * gain).astype(BF))
        square = jnp.sum(m * m, axis=1, keepdims=True)
        SR[0, 4:8, ts] = jnp.broadcast_to(square, (T, T)).T[0:4, :]
    for o in range(16):
        if o:
            dk = o // 8
            send(
                SR.at[0], SR.at[o], sx_s.at[o], sx_r.at[o],
                sibling if dk else c, y * 8 + zz(o % 8),
            )

    lc_wi.wait()
    arrive(WI.at[1 - k], sib_s.at[2], sib_r.at[2])

    def ffn_in(o, first=False):
        zs = zz(o)
        ws = cols(pos(zs), FB)

        def body(i, carry):
            rows = pl.ds(pl.multiple_of(i * 160, 16), 160)
            xb = XG[zs, rows, :]
            for q in range(4):
                r = nt(xb, WI[q // 2, q % 2, :, ws])
                if first:
                    ACC[q, rows, :] = r
                else:
                    ACC[q, rows, :] = ACC[q, rows, :] + r
            return carry
        lax.fori_loop(0, 4, body, 0)

    for h in range(1, 5):
        for r in range(2):
            if h <= HOPB[r]:
                arrive(piece_b(zz(-step_dir[r] * h), 0), br_s.at[r, h - 1], br_r.at[r, h - 1])
                if h < HOPB[r]:
                    beta_ring(r, h + 1)
                beta_x(-step_dir[r] * h)
        for d in range(4):
            if h == 1 and d:
                arrive(piece_a(z, d), ax_s.at[d - 1], ax_r.at[d - 1])
                alpha_ring(0, d, 1)
                alpha_ring(1, d, 1)
        for d in range(4):
            for r in range(2):
                if h <= HOPS[r][d]:
                    arrive(
                        piece_a(zz(-step_dir[r] * h), d),
                        ar_s.at[r, d, h - 1], ar_r.at[r, d, h - 1],
                    )
                    if h < HOPS[r][d]:
                        alpha_ring(r, d, h + 1)
        if h == 1:
            beta_x_wait(0)
            ffn_in(0, True)
        else:
            for o in (h - 1, 1 - h):
                beta_x_wait(o)
                ffn_in(o)
        if h == 3:
            for o in range(1, 16):
                arrive(SR.at[o], sx_s.at[o], sx_r.at[o])
            tot = SR[0]
            for o in range(1, 16):
                tot = tot + SR[o]
            rstd = lax.rsqrt(tot[4:5, :] / D + EPS)
            LG[...] = tot * rstd
            rs = jnp.concatenate(
                [
                    nt(jnp.broadcast_to(rstd[:, kc * T:(kc + 1) * T], (8, T)), PL[kc], HI)
                    for kc in range(2)
                ],
                axis=1,
            )
            RX[0] = rs
            for d in range(1, 4):
                send(RX.at[0], RX.at[d], rx_s.at[d - 1], rx_r.at[d - 1], 2 * xx(d) + k, e)
    beta_x_wait(-4)
    ws4 = cols(pos(zz(4)), FB)

    def last(i, carry):
        rows = pl.ds(pl.multiple_of(i * 160, 16), 160)
        for g in range(2):
            r = nt(XG[zz(4), rows, :], WI[1 - k, g, :, ws4])
            PS[g, rows, :] = (ACC[2 * (1 - k) + g, rows, :] + r).astype(BF)
        return carry
    lax.fori_loop(0, 4, last, 0)

    send(PS, PR, pr_s.at[0], pr_r.at[0], sibling, e)

    def last_own(i, carry):
        rows = pl.ds(pl.multiple_of(i * 160, 16), 160)
        for g in range(2):
            r = nt(XG[zz(4), rows, :], WI[k, g, :, ws4])
            ACC[2 * k + g, rows, :] = ACC[2 * k + g, rows, :] + r
        return carry
    lax.fori_loop(0, 4, last_own, 0)
    for kc in range(2):
        sg = 1.0 / (1.0 + jnp.exp(-LG[:, kc * T:(kc + 1) * T]))
        i0, i1 = IDS[kc, 0:1, :], IDS[kc, 1:2, :]
        den = jnp.zeros((1, T), F32)
        num = jnp.zeros((1, T), F32)
        for j in range(4):
            hit = ((i0 == j) | (i1 == j)).astype(F32) * sg[j:j + 1, :]
            den = den + hit
            num = num + jnp.where(y == j, hit, 0.0)
        GC[kc] = jnp.broadcast_to(num / den, (T, T)).T
        PT[kc] = PL[kc].T[:, :CAP].astype(BF)
    for d in range(1, 4):
        arrive(RX.at[d], rx_s.at[d - 1], rx_r.at[d - 1])
    lc_wd.wait()
    arrive(WD.at[1 - k], sib_s.at[3], sib_r.at[3])
    arrive(PR, pr_s.at[0], pr_r.at[0])
    for d in range(4):
        for kc in range(2):
            rs = RX[d, 0:1, kc * T:(kc + 1) * T]
            col = jnp.broadcast_to(rs, (T, T)).T[:CAP, 0:1]
            rows = (rows_b if kc else rows_a)(xx(-d))
            g = (ACC[2 * k, rows, :] + PR[0, rows, :].astype(F32)) * col
            u = (ACC[2 * k + 1, rows, :] + PR[1, rows, :].astype(F32)) * col
            HID[k, rows, :] = (g / (1.0 + jnp.exp(-g)) * u).astype(BF)
        part = HID.at[k, pl.ds(pl.multiple_of(xx(-d) * 160, 16), 160)]
        send(part, part, pr_s.at[1 + d], pr_r.at[1 + d], sibling, e)
    for d in range(4):
        part = HID.at[1 - k, pl.ds(pl.multiple_of(xx(-d) * 160, 16), 160)]
        arrive(part, pr_s.at[1 + d], pr_r.at[1 + d])

    def down(o):
        zs = zz(o)
        ws = cols(pos(zs), FB)

        def body(i, carry):
            rows = pl.ds(pl.multiple_of(i * 160, 16), 160)
            r = nn(HID[0, rows, :], WD[0, :, ws]) + nn(HID[1, rows, :], WD[1, :, ws])
            YY[zs, rows, :] = r.astype(BF)
            return carry
        lax.fori_loop(0, 4, body, 0)

    def back_ring(r, d, s):
        hops = HOPS[r][d]
        zs = zz(step_dir[r] * (hops - s))
        p = YY.at[zs, rows_a(xx(d))]
        if s:
            arrive(RBA.at[r, d, s - 1], rr_s.at[r, d, s - 1], rr_r.at[r, d, s - 1])
            p[...] = (p[...].astype(F32) + RBA[r, d, s - 1].astype(F32)).astype(BF)
        send(p, RBA.at[r, d, s], rr_s.at[r, d, s], rr_r.at[r, d, s], c, y * 8 + zz(step_dir[r]))

    def back_x(o):
        for d in range(1, 4):
            send(
                YY.at[zz(o), rows_b(xx(d))], XRB.at[o % 8, d - 1],
                rx2_s.at[o % 8, d - 1], rx2_r.at[o % 8, d - 1], 2 * xx(d) + k, e,
            )

    def back_x_sum(o):
        acc = YY[zz(o), rows_b(x), :].astype(F32)
        for d in range(1, 4):
            arrive(XRB.at[o % 8, d - 1], rx2_s.at[o % 8, d - 1], rx2_r.at[o % 8, d - 1])
            acc = acc + XRB[o % 8, d - 1].astype(F32)
        return acc

    def back_ring_b(r, s):
        o = step_dir[r] * (HOPB[r] - s)
        acc = back_x_sum(o)
        if s:
            arrive(RBB.at[r, s - 1], rb_s.at[r, s - 1], rb_r.at[r, s - 1])
            acc = acc + RBB[r, s - 1].astype(F32)
        p = YY.at[zz(o), rows_b(x)]
        p[...] = acc.astype(BF)
        send(p, RBB.at[r, s], rb_s.at[r, s], rb_r.at[r, s], c, y * 8 + zz(step_dir[r]))

    for o in (4, 3, -3, -2, 2, -1, 1, 0):
        down(o)
        for r in range(2):
            for d in range(4):
                if (step_dir[r] * HOPS[r][d] - o) % 8 == 0:
                    back_ring(r, d, 0)
        back_x(o)
    for s in range(1, 4):
        for d in (2, 1, 3, 0):
            for r in range(2):
                if s < HOPS[r][d]:
                    back_ring(r, d, s)
        for r in range(2):
            back_ring_b(r, s - 1)
    for d in (2, 1, 3, 0):
        acc = YY[z, rows_a(xx(d)), :].astype(F32)
        for r in range(2):
            s = HOPS[r][d] - 1
            arrive(RBA.at[r, d, s], rr_s.at[r, d, s], rr_r.at[r, d, s])
            acc = acc + RBA[r, d, s].astype(F32)
        if d:
            p = YY.at[z, rows_a(xx(d))]
            p[...] = acc.astype(BF)
            send(p, XRA.at[d - 1], ra_s.at[d - 1], ra_r.at[d - 1], 2 * xx(d) + k, e)
        else:
            YS[0, :, :] = acc
    back_ring_b(0, 3)
    acc = back_x_sum(0)
    for r in range(2):
        s = HOPB[r] - 1
        arrive(RBB.at[r, s], rb_s.at[r, s], rb_r.at[r, s])
        acc = acc + RBB[r, s].astype(F32)
    YS[1, :, :] = acc
    acc = YS[0, :, :]
    for d in range(1, 4):
        arrive(XRA.at[d - 1], ra_s.at[d - 1], ra_r.at[d - 1])
        acc = acc + XRA[d - 1].astype(F32)
    YS[0, :, :] = acc

    first = (y == 0).astype(F32)
    target = 2 * b
    for kc in range(2):
        got = nn(PT[kc], YS[kc].astype(BF))
        got = got * GC[kc, :, 0:1] + first * MID[kc]
        for j in range(2):
            FS[kc * 2 + j] = got[:, j * OUT:(j + 1) * OUT].astype(BF)
            dc, de = 2 * x + kc, target + j
            is_me = (k == kc) & (de == e)

            @pl.when(is_me)
            def _(i=kc * 2 + j):
                FR[y] = FS[i]

            @pl.when(jnp.logical_not(is_me))
            def _(i=kc * 2 + j, dc=dc, de=de):
                send(FS.at[i], FR.at[y], fn_s.at[i], fn_r.at[y], dc, de, False)

    for yy in range(4):
        @pl.when(jnp.logical_not(src_mine & (y == yy)))
        def _(yy=yy):
            arrive(FR.at[yy], fn_s.at[yy], fn_r.at[yy])
    acc = FR[0].astype(F32)
    for yy in range(1, 4):
        acc = acc + FR[yy].astype(F32)
    out_ref[...] = acc.astype(BF)

    def left(src, ss):
        pltpu.make_async_remote_copy(
            src_ref=src, dst_ref=src, send_sem=ss, recv_sem=ss,
            device_id=(c, e), device_id_type=MESH,
        ).wait_send()

    for cp in pend:
        cp.wait_send()
    for d in range(1, 4):
        @pl.when(x + d < 4)
        def _(d=d):
            left(TC, tt_s.at[d])
            left(LC, st_s.at[d])
    for kc in range(2):
        @pl.when(k != kc)
        def _(kc=kc):
            left(QQ.at[:, cols(kc * 8 + pos(z), FY)], a2_s.at[kc, 0])
            left(PZ.at[:, cols(kc * 8 + pos(z), FZ)], z1_s.at[kc, 0])
        for j in range(2):
            @pl.when(jnp.logical_not((k == kc) & (target + j == e)))
            def _(i=kc * 2 + j):
                left(FS.at[i], fn_s.at[i])


def local(tok, q, kk, v, ld, inc, ag, wo, fg, ro, ids, wi, wd):
    vm = lambda *s, t=BF: pltpu.VMEM(s, t)
    dma = lambda *s: pltpu.SemaphoreType.DMA(s)
    inside = pl.BlockSpec(memory_space=pltpu.VMEM)
    outside = pl.BlockSpec(memory_space=pl.ANY)
    scratch = [
        vm(256, D), vm(2, 2, SL, HALF), vm(2, SL, HALF), vm(2, T, FB), vm(2, 8, T, t=F32),
        vm(2, HD, HD, t=F32), vm(2, HD, HD), vm(8, T, t=F32), vm(4, HD, HD), vm(4, 8, T, t=F32),
        vm(2, HD, HD, t=F32), vm(HD, HD, t=F32), vm(HD, HD), vm(8, T, t=F32),
        vm(2, T, HD, t=F32), vm(2, T, HD, t=F32), vm(8, T, t=F32),
        vm(T, 2 * HD), vm(T, DY), vm(T, D - DY), vm(3, 32, DY), vm(32, DY), vm(2, 8, 32, FY),
        vm(2, 8, T, FZ), vm(2, T, FZ), vm(3, 2, 32, FZ), vm(4, 2, 32, FB),
        vm(2, T, FB, t=F32),
        vm(2, T, T, t=F32), vm(2, T, CAP), vm(2, T, T, t=F32), vm(16, 8, 2 * T, t=F32), vm(8, 2 * T, t=F32), vm(4, 8, 2 * T, t=F32), vm(8, 8 * CAP, FB),
        vm(4, 8 * CAP, SL, t=F32), vm(2, 8 * CAP, SL), vm(2, 8 * CAP, SL), vm(2, 8 * CAP, SL),
        vm(8, 8 * CAP, FB), vm(2, 4, 4, CAP, FB), vm(2, 4, CAP, FB), vm(3, CAP, FB), vm(8, 3, CAP, FB),
        vm(2, CAP, FB, t=F32), vm(4, T, OUT), vm(4, T, OUT),
        dma(5), dma(4), dma(4), dma(4), dma(4), dma(5), dma(5),
        dma(6), dma(6), dma(2, 8), dma(2, 8), dma(3), dma(3), dma(2, 8), dma(2, 8), dma(3), dma(3), dma(16), dma(16), dma(3), dma(3),
        dma(5), dma(5), dma(3), dma(3), dma(2, 4, 4), dma(2, 4, 4), dma(2, 4), dma(2, 4), dma(8, 3), dma(8, 3),
        dma(3), dma(3), dma(2, 4, 4), dma(2, 4, 4), dma(2, 4), dma(2, 4), dma(8, 3), dma(8, 3), dma(4), dma(4),
    ]
    return pl.pallas_call(
        kernel,
        out_shape=jax.ShapeDtypeStruct((T, OUT), BF),
        in_specs=[
            outside, inside, inside, inside, inside, inside, inside,
            outside, inside, inside, inside, outside, outside,
        ],
        out_specs=inside,
        scratch_shapes=scratch,
        compiler_params=pltpu.CompilerParams(
            collective_id=0, has_side_effects=True, vmem_limit_bytes=56 * 2**20
        ),
        cost_estimate=pl.CostEstimate(flops=4 * 10**9, bytes_accessed=10**7, transcendentals=10**5),
    )(tok, q, kk, v, ld, inc, ag.reshape(2, HD), wo, fg.reshape(D // 128, 128), ro.T, ids.T, wi, wd)


def solution(mesh):
    return jax.shard_map(
        local,
        mesh=mesh,
        in_specs=(
            P("ctx", None),
            P("ctx", "exp"),
            P("ctx", "exp"),
            P("ctx", "exp"),
            P("exp", "ctx"),
            P("exp", None, None),
            P("exp"),
            P("exp", None),
            P(),
            P(),
            P("ctx", None),
            P(None, ("exp", "ctx"), None),
            P(("exp", "ctx"), None),
        ),
        out_specs=P("ctx", "exp"),
        check_vma=False,
    )
```

```python
import functools

import jax
import jax.numpy as jnp
from jax import lax
from jax.experimental import pallas as pl
from jax.experimental.pallas import tpu as pltpu
from jax.sharding import PartitionSpec as P

MESH = pl.DeviceIdType.MESH
HI = lax.Precision.HIGHEST
F32 = jnp.float32
BF = jnp.bfloat16
EPS = 1e-06

D = 6144
T = 128
HD = 128
CAP = 80
SL = 144
HALF = D // 2
FB = HALF // 8
OUT = D // 32
FZ = 128
FY = FB - FZ
DY = 16 * FY

HOPS = ((4, 4, 3, 3), (3, 3, 4, 4))
HOPB = (4, 3)
NG = 64
NR = 64


def nt(a, b, precision=None):
    return lax.dot_general(
        a, b, (((1,), (1,)), ((), ())), preferred_element_type=F32, precision=precision
    )


def nn(a, b, precision=None):
    return jnp.dot(a, b, preferred_element_type=F32, precision=precision)


def iota2(shape, dim):
    return lax.broadcasted_iota(jnp.int32, shape, dim)


def kernel(
    tok_ref,
    q_ref,
    k_ref,
    v_ref,
    ld_ref,
    inc_ref,
    ag_ref,
    wo_ref,
    fg_ref,
    ro_ref,
    ids_ref,
    wi_ref,
    wd_ref,
    out_ref,
    WO, WI, WD, TK, IDS,
    LF, LS, TS, LB, TB, ST, SO, LC, TC, IN, QS, WR,
    AH, PP, PZ, A1R, QQ, A2R, Z1R, ZQ, Z2R, A3R, MID,
    PL, PT, GC, SR, LG, RX, XG, ACC, PS, PR, HID,
    YY, RBA, RBB, XRA, XRB, YS, FS, FR,
    loc, sib_s, sib_r, st_s, st_r, tt_s, tt_r,
    a1_s, a1_r, z1_s, z1_r, z2_s, z2_r, a2_s, a2_r, a3_s, a3_r, sx_s, sx_r, rx_s, rx_r,
    pr_s, pr_r, ax_s, ax_r, ar_s, ar_r, br_s, br_r, bx_s, bx_r,
    ra_s, ra_r, rr_s, rr_r, rb_s, rb_r, rx2_s, rx2_r, fn_s, fn_r,
):
    c = lax.axis_index("ctx")
    e = lax.axis_index("exp")
    x, k = c // 2, lax.rem(c, 2)
    y, z = e // 8, lax.rem(e, 8)

    def pos(zs):
        return lax.rem(zs, 2) * 4 + zs // 2

    b = k * 8 + pos(z)
    pend = []

    def xx(d):
        return lax.rem(x + (d + 8), 4)

    def yv(d):
        return lax.rem(y + (d + 8), 4)

    def zz(o):
        return lax.rem(z + (o + 16), 8)

    def send(src, dst, ss, rs, dc, de, keep=True):
        cp = pltpu.make_async_remote_copy(
            src_ref=src, dst_ref=dst, send_sem=ss, recv_sem=rs,
            device_id=(dc, de), device_id_type=MESH,
        )
        cp.start()
        if keep:
            pend.append(cp)
        return cp

    def arrive(dst, ss, rs):
        pltpu.make_async_remote_copy(
            src_ref=dst, dst_ref=dst, send_sem=ss, recv_sem=rs,
            device_id=(c, e), device_id_type=MESH,
        ).wait_recv()

    def cols(i, n):
        return pl.ds(pl.multiple_of(i * n, 128), n)

    bar = pltpu.get_barrier_semaphore()

    def hello(dc, de):
        pl.semaphore_signal(bar, inc=1, device_id=(dc, de), device_id_type=MESH)

    sibling = 2 * x + (1 - k)
    hello(sibling, e)
    for d in range(1, 4):
        hello(2 * xx(d) + k, e)
    for d in range(1, 4):
        hello(c, yv(d) * 8 + z)
    for o in (4, 3, 5, 2, 6, 1, 7):
        hello(c, y * 8 + zz(o))
        hello(sibling, y * 8 + zz(o))
    src_b = e // 2
    src_k, src_p = src_b // 8, lax.rem(src_b, 8)
    src_z = 2 * lax.rem(src_p, 4) + src_p // 4
    src_mine = (src_k == k) & (src_z == z)
    for yy in range(4):
        @pl.when(jnp.logical_not(src_mine & (y == yy)))
        def _(yy=yy):
            hello(2 * x + src_k, yy * 8 + src_z)
    lc_wo = pltpu.make_async_copy(wo_ref, WO, loc.at[0])
    lc_wo.start()
    lc_tk = pltpu.make_async_copy(tok_ref.at[:, cols(b, FB)], TK.at[k], loc.at[1])
    lc_tk.start()

    row_i = iota2((T, T), 0)
    col_i = iota2((T, T), 1)
    lower = row_i >= col_i
    scale = HD ** (-0.5)
    cums = []
    for h in range(2):
        hs = slice(h * HD, (h + 1) * HD)
        ld = ld_ref[h:h + 1, :]
        cum = jnp.sum(jnp.where(lower, ld, 0.0), axis=1, keepdims=True)
        tot = jnp.sum(ld, axis=1, keepdims=True)
        cums.append(cum)
        ks = k_ref[:, hs].astype(F32) * jnp.exp(tot - cum)
        LF[h] = nn(ks.T, v_ref[:, hs].astype(F32), HI)
        LS[h] = LF[h].astype(BF)
        TS[h:h + 1, :] = jnp.broadcast_to(tot, (1, T))
    TS[2:, :] = jnp.zeros((6, T), F32)
    IDS[k, 0:2, :] = ids_ref[...].astype(F32)
    IDS[k, 2:8, :] = jnp.zeros((6, T), F32)

    pl.semaphore_wait(bar, 25 - (src_mine).astype(jnp.int32))

    send(TS, TB.at[0], tt_s.at[0], tt_r.at[0], sibling, e)
    send(LS.at[1 - k], LB.at[0], st_s.at[0], st_r.at[0], sibling, e)
    ob = (1 - k) * 8 + pos(z)
    send(tok_ref.at[:, cols(ob, FB)], TK.at[k], sib_s.at[0], sib_r.at[0], sibling, e)
    send(IDS.at[k], IDS.at[k], sib_s.at[1], sib_r.at[1], sibling, e)
    mine, other = cols(k, HALF), cols(1 - k, HALF)
    lc_wi = pltpu.make_async_copy(wi_ref.at[:, :, mine], WI.at[k], loc.at[3])
    lc_wi.start()
    lc_wd = pltpu.make_async_copy(wd_ref.at[:, mine], WD.at[k], loc.at[4])
    lc_wd.start()
    send(wi_ref.at[:, :, other], WI.at[k], sib_s.at[2], sib_r.at[2], sibling, e)
    send(wd_ref.at[:, other], WD.at[k], sib_s.at[3], sib_r.at[3], sibling, e)

    arrive(TB.at[0], tt_s.at[0], tt_r.at[0])
    arrive(LB.at[0], st_s.at[0], st_r.at[0])
    mine_l, other_l = LF[k], LB[0].astype(F32)
    mine_t, other_t = TS[pl.ds(k, 1), :], TB[0, pl.ds(k, 1), :]
    core0 = k == 0
    l0 = jnp.where(core0, mine_l, other_l)
    l1 = jnp.where(core0, other_l, mine_l)
    t0 = jnp.where(core0, mine_t, other_t)
    t1 = jnp.where(core0, other_t, mine_t)
    LC[...] = (jnp.exp(t1) * l0 + l1).astype(BF)
    TC[...] = jnp.broadcast_to(t0 + t1, (8, T))
    for d in range(1, 4):
        @pl.when(x + d < 4)
        def _(d=d):
            send(TC, TB.at[d], tt_s.at[d], tt_r.at[d], c + 2 * d, e, False)
            send(LC, LB.at[d], st_s.at[d], st_r.at[d], c + 2 * d, e, False)

    for h in range(2):
        hs = slice(h * HD, (h + 1) * HD)
        cum = cums[h]
        cb = jnp.broadcast_to(cum, (T, T))
        gap = jnp.where(lower, cb - cb.T, 0.0)
        weight = jnp.where(lower, jnp.exp(gap), 0.0)
        sc = nt(q_ref[:, hs], k_ref[:, hs]) * scale * weight
        IN[h] = nn(sc, v_ref[:, hs].astype(F32), HI)
        QS[h] = q_ref[:, hs].astype(F32) * (scale * jnp.exp(cum))

    ST[k] = jnp.zeros((HD, HD), F32)
    WR[...] = jnp.zeros_like(WR)
    for d in range(1, 4):
        @pl.when(x >= d)
        def _(d=d):
            arrive(TB.at[d], tt_s.at[d], tt_r.at[d])
            arrive(LB.at[d], st_s.at[d], st_r.at[d])
            ST[k] = ST[k] + jnp.exp(WR[0:1, :]) * LB[d].astype(F32)
            WR[...] = WR[...] + TB[d]
    start = ST[k] + jnp.exp(WR[0:1, :]) * inc_ref[k]
    after = jnp.exp(t0) * start + l0
    ST[k] = jnp.where(core0, start, after)
    SO[...] = jnp.where(core0, after, start)
    send(SO, ST.at[k], tt_s.at[4], tt_r.at[4], sibling, e)

    def finish(h):
        att = IN[h] + nn(QS[h], ST[h], HI)
        ms = jnp.mean(att * att, axis=1, keepdims=True)
        AH[:, pl.ds(pl.multiple_of(h * HD, HD), HD)] = (
            att * lax.rsqrt(ms + EPS) * ag_ref[pl.ds(h, 1), :]
        ).astype(BF)

    finish(k)
    arrive(ST.at[1 - k], tt_s.at[4], tt_r.at[4])
    finish(1 - k)

    lc_wo.wait()
    for kc in range(2):
        def project(i, carry, kc=kc):
            bl = kc * 8 + i
            r = nn(AH[...], WO[:, cols(bl, FB)]).astype(BF)
            PP[:, cols(bl, FY)] = r[:, :FY]
            PZ[:, cols(bl, FZ)] = r[:, FY:]
            return carry
        lax.fori_loop(0, 8, project, 0)
        cs = slice(kc * 8 * FY, (kc + 1) * 8 * FY)
        for d in (2, 1, 3):
            i = kc * 3 + d - 1
            send(
                PP.at[pl.ds(pl.multiple_of(yv(d) * 32, 32), 32), cs],
                A1R.at[d - 1, :, cs],
                a1_s.at[i], a1_r.at[i], c, yv(d) * 8 + z,
            )
        dest = 2 * x + kc
        for o in (4, 3, 5, 2, 6, 1, 7):
            send(
                PZ.at[:, cols(kc * 8 + pos(zz(o)), FZ)],
                Z1R.at[k, o], z1_s.at[kc, o], z1_r.at[k, o], dest, y * 8 + zz(o),
            )
        own = cols(kc * 8 + pos(z), FZ)

        @pl.when(k == kc)
        def _(own=own):
            Z1R[k, 0] = PZ[:, own]

        @pl.when(k != kc)
        def _(own=own, kc=kc, dest=dest):
            send(PZ.at[:, own], Z1R.at[k, 0], z1_s.at[kc, 0], z1_r.at[k, 0], dest, e, False)
    for kc in range(2):
        cs = slice(kc * 8 * FY, (kc + 1) * 8 * FY)
        for d in range(1, 4):
            i = kc * 3 + d - 1
            arrive(A1R.at[d - 1, :, cs], a1_s.at[i], a1_r.at[i])

        def add_y(i, carry, kc=kc):
            s = pl.ds(pl.multiple_of(kc * 8 * FY + i * 512, 128), 512)
            acc = PP[pl.ds(pl.multiple_of(y * 32, 32), 32), s].astype(F32)
            for d in range(3):
                acc = acc + A1R[d, :, s].astype(F32)
            QQ[:, s] = acc.astype(BF)
            return carry
        lax.fori_loop(0, 8 * FY // 512, add_y, 0)
        dest = 2 * x + kc
        for o in (4, 3, 5, 2, 6, 1, 7):
            send(
                QQ.at[:, cols(kc * 8 + pos(zz(o)), FY)],
                A2R.at[k, o], a2_s.at[kc, o], a2_r.at[k, o], dest, y * 8 + zz(o),
            )
        own = cols(kc * 8 + pos(z), FY)

        @pl.when(k == kc)
        def _(own=own):
            A2R[k, 0] = QQ[:, own]

        @pl.when(k != kc)
        def _(own=own, kc=kc, dest=dest):
            send(QQ.at[:, own], A2R.at[k, 0], a2_s.at[kc, 0], a2_r.at[k, 0], dest, e, False)

    for kc in range(2):
        @pl.when(k != kc)
        def _(kc=kc):
            arrive(Z1R.at[kc, 0], z1_s.at[kc, 0], z1_r.at[kc, 0])
        acc = Z1R[kc, 0].astype(F32)
        for o in range(1, 8):
            arrive(Z1R.at[kc, o], z1_s.at[kc, o], z1_r.at[kc, o])
            acc = acc + Z1R[kc, o].astype(F32)
        ZQ[kc] = acc.astype(BF)
    for d in (2, 1, 3):
        send(
            ZQ.at[:, pl.ds(pl.multiple_of(yv(d) * 32, 32), 32)], Z2R.at[d - 1],
            z2_s.at[d - 1], z2_r.at[d - 1], c, yv(d) * 8 + z,
        )
    for kc in range(2):
        @pl.when(k != kc)
        def _(kc=kc):
            arrive(A2R.at[kc, 0], a2_s.at[kc, 0], a2_r.at[kc, 0])
        acc = A2R[kc, 0].astype(F32)
        for o in range(1, 8):
            arrive(A2R.at[kc, o], a2_s.at[kc, o], a2_r.at[kc, o])
            acc = acc + A2R[kc, o].astype(F32)
        A3R[0, kc, :, :FY] = acc.astype(BF)
    acc = ZQ[:, pl.ds(pl.multiple_of(y * 32, 32), 32), :].astype(F32)
    for d in range(1, 4):
        arrive(Z2R.at[d - 1], z2_s.at[d - 1], z2_r.at[d - 1])
        acc = acc + Z2R[d - 1].astype(F32)
    A3R[0, :, :, FY:] = acc.astype(BF)
    for d in range(1, 4):
        send(A3R.at[0], A3R.at[d], a3_s.at[d - 1], a3_r.at[d - 1], c, yv(d) * 8 + z)

    arrive(IDS.at[1 - k], sib_s.at[1], sib_r.at[1])
    strict = (row_i < col_i).astype(BF)
    yf = y.astype(F32)
    for kc in range(2):
        mask = ((IDS[kc, 0:1, :] == yf) | (IDS[kc, 1:2, :] == yf)).astype(F32)
        before = nn(jnp.broadcast_to(mask, (8, T)).astype(BF), strict)[0:1, :]
        PL[kc] = jnp.where(
            (row_i.astype(F32) == before) & (row_i < CAP), mask, 0.0
        )

    lc_tk.wait()
    arrive(TK.at[1 - k], sib_s.at[0], sib_r.at[0])
    gain = jnp.concatenate([fg_ref[pl.ds(b * 3 + i, 1), :] for i in range(3)], axis=1)
    for d in range(4):
        if d:
            arrive(A3R.at[d], a3_s.at[d - 1], a3_r.at[d - 1])
        rows = pl.ds(pl.multiple_of(yv(-d) * 32, 32), 32)
        for kc in range(2):
            MID[kc, rows, :] = TK[kc, rows, :].astype(F32) + A3R[d, kc].astype(F32)

    def rows_a(i, n=NG):
        return pl.ds(pl.multiple_of(i * 160, 16), n)

    def rows_b(i, n=NG):
        return pl.ds(pl.multiple_of(i * 160 + n, 16), 160 - n)

    def slot_rows(i, kc):
        return pl.ds(pl.multiple_of(i * 160 + 80 * kc, 16), 80)

    def piece_a(zs, d):
        return XG.at[zs, rows_a(xx(-d))]

    def piece_b(zs, d):
        return XG.at[zs, rows_b(xx(-d))]

    step_dir = (1, -1)

    def alpha_ring(r, d, h):
        p = piece_a(zz(-step_dir[r] * (h - 1)), d)
        send(p, p, ar_s.at[r, d, h - 1], ar_r.at[r, d, h - 1], c, y * 8 + zz(step_dir[r]))

    def beta_ring(r, h):
        p = piece_b(zz(-step_dir[r] * (h - 1)), 0)
        send(p, p, br_s.at[r, h - 1], br_r.at[r, h - 1], c, y * 8 + zz(step_dir[r]))

    def beta_x(o):
        p = piece_b(zz(o), 0)
        for d in range(1, 4):
            send(p, p, bx_s.at[o % 8, d - 1], bx_r.at[o % 8, d - 1], 2 * xx(d) + k, e)

    def beta_x_wait(o):
        for d in range(1, 4):
            arrive(piece_b(zz(o), d), bx_s.at[o % 8, d - 1], bx_r.at[o % 8, d - 1])

    for kc in (1, 0):
        xg = (MID[kc] * gain).astype(BF)
        slots = nn(PL[kc, :CAP, :].astype(BF), xg).astype(BF)
        XG[z, slot_rows(x, kc), :] = slots
        if kc and NG >= 80:
            beta_ring(0, 1)
            beta_ring(1, 1)
    if NG < 80:
        beta_ring(0, 1)
        beta_ring(1, 1)
    pa = piece_a(z, 0)
    for d in range(1, 4):
        send(pa, pa, ax_s.at[d - 1], ax_r.at[d - 1], 2 * xx(d) + k, e)
    alpha_ring(0, 0, 1)
    alpha_ring(1, 0, 1)
    beta_x(0)
    lc_wi.wait()
    arrive(WI.at[1 - k], sib_s.at[2], sib_r.at[2])

    def ffn_in(o, first=False):
        zs = zz(o)
        ws = cols(pos(zs), FB)

        def body(i, carry):
            rows = pl.ds(pl.multiple_of(i * 160, 16), 160)
            xb = XG[zs, rows, :]
            for q in range(4):
                r = nt(xb, WI[q // 2, q % 2, :, ws])
                if first:
                    ACC[q, rows, :] = r
                else:
                    ACC[q, rows, :] = ACC[q, rows, :] + r
            return carry
        lax.fori_loop(0, 4, body, 0)

    for h in range(1, 5):
        for r in range(2):
            if h <= HOPB[r]:
                arrive(piece_b(zz(-step_dir[r] * h), 0), br_s.at[r, h - 1], br_r.at[r, h - 1])
                if h < HOPB[r]:
                    beta_ring(r, h + 1)
                beta_x(-step_dir[r] * h)
        for d in range(4):
            if h == 1 and d:
                arrive(piece_a(z, d), ax_s.at[d - 1], ax_r.at[d - 1])
                alpha_ring(0, d, 1)
                alpha_ring(1, d, 1)
        for d in range(4):
            for r in range(2):
                if h <= HOPS[r][d]:
                    arrive(
                        piece_a(zz(-step_dir[r] * h), d),
                        ar_s.at[r, d, h - 1], ar_r.at[r, d, h - 1],
                    )
                    if h < HOPS[r][d]:
                        alpha_ring(r, d, h + 1)
        if h == 1:
            beta_x_wait(0)
            ffn_in(0, True)
        else:
            for o in (h - 1, 1 - h):
                beta_x_wait(o)
                ffn_in(o)
        if h == 2:
            router = ro_ref[:, cols(b, FB)]
            for kc in range(2):
                m = MID[kc]
                ts = slice(kc * T, (kc + 1) * T)
                SR[0, 0:4, ts] = nt(router, (m * gain).astype(BF))
                square = jnp.sum(m * m, axis=1, keepdims=True)
                SR[0, 4:8, ts] = jnp.broadcast_to(square, (T, T)).T[0:4, :]
            for o in range(16):
                if o:
                    dk = o // 8
                    send(
                        SR.at[0], SR.at[o], sx_s.at[o], sx_r.at[o],
                        sibling if dk else c, y * 8 + zz(o % 8),
                    )

        if h == 4:
            for o in range(1, 16):
                arrive(SR.at[o], sx_s.at[o], sx_r.at[o])
            tot = SR[0]
            for o in range(1, 16):
                tot = tot + SR[o]
            rstd = lax.rsqrt(tot[4:5, :] / D + EPS)
            LG[...] = tot * rstd
            rs = jnp.concatenate(
                [
                    nt(jnp.broadcast_to(rstd[:, kc * T:(kc + 1) * T], (8, T)), PL[kc], HI)
                    for kc in range(2)
                ],
                axis=1,
            )
            RX[0] = rs
            for d in range(1, 4):
                send(RX.at[0], RX.at[d], rx_s.at[d - 1], rx_r.at[d - 1], 2 * xx(d) + k, e)
    beta_x_wait(-4)
    ws4 = cols(pos(zz(4)), FB)

    def last(i, carry):
        rows = pl.ds(pl.multiple_of(i * 160, 16), 160)
        for g in range(2):
            r = nt(XG[zz(4), rows, :], WI[1 - k, g, :, ws4])
            PS[g, rows, :] = (ACC[2 * (1 - k) + g, rows, :] + r).astype(BF)
        return carry
    lax.fori_loop(0, 4, last, 0)

    send(PS, PR, pr_s.at[0], pr_r.at[0], sibling, e)

    def last_own(i, carry):
        rows = pl.ds(pl.multiple_of(i * 160, 16), 160)
        for g in range(2):
            r = nt(XG[zz(4), rows, :], WI[k, g, :, ws4])
            ACC[2 * k + g, rows, :] = ACC[2 * k + g, rows, :] + r
        return carry
    lax.fori_loop(0, 4, last_own, 0)
    for kc in range(2):
        sg = 1.0 / (1.0 + jnp.exp(-LG[:, kc * T:(kc + 1) * T]))
        i0, i1 = IDS[kc, 0:1, :], IDS[kc, 1:2, :]
        den = jnp.zeros((1, T), F32)
        num = jnp.zeros((1, T), F32)
        for j in range(4):
            hit = ((i0 == j) | (i1 == j)).astype(F32) * sg[j:j + 1, :]
            den = den + hit
            num = num + jnp.where(y == j, hit, 0.0)
        GC[kc] = jnp.broadcast_to(num / den, (T, T)).T
        PT[kc] = PL[kc].T[:, :CAP].astype(BF)
    for d in range(1, 4):
        arrive(RX.at[d], rx_s.at[d - 1], rx_r.at[d - 1])
    lc_wd.wait()
    arrive(WD.at[1 - k], sib_s.at[3], sib_r.at[3])
    arrive(PR, pr_s.at[0], pr_r.at[0])
    for d in range(4):
        for kc in range(2):
            rs = RX[d, 0:1, kc * T:(kc + 1) * T]
            col = jnp.broadcast_to(rs, (T, T)).T[:CAP, 0:1]
            rows = slot_rows(xx(-d), kc)
            g = (ACC[2 * k, rows, :] + PR[0, rows, :].astype(F32)) * col
            u = (ACC[2 * k + 1, rows, :] + PR[1, rows, :].astype(F32)) * col
            HID[k, rows, :] = (g / (1.0 + jnp.exp(-g)) * u).astype(BF)
        part = HID.at[k, pl.ds(pl.multiple_of(xx(-d) * 160, 16), 160)]
        send(part, part, pr_s.at[1 + d], pr_r.at[1 + d], sibling, e)
    for d in range(4):
        part = HID.at[1 - k, pl.ds(pl.multiple_of(xx(-d) * 160, 16), 160)]
        arrive(part, pr_s.at[1 + d], pr_r.at[1 + d])

    def down(o):
        zs = zz(o)
        ws = cols(pos(zs), FB)

        def body(i, carry):
            rows = pl.ds(pl.multiple_of(i * 160, 16), 160)
            r = nn(HID[0, rows, :], WD[0, :, ws]) + nn(HID[1, rows, :], WD[1, :, ws])
            YY[zs, rows, :] = r.astype(BF)
            return carry
        lax.fori_loop(0, 4, body, 0)

    def back_ring(r, d, s):
        hops = HOPS[r][d]
        zs = zz(step_dir[r] * (hops - s))
        p = YY.at[zs, rows_a(xx(d), NR)]
        if s:
            arrive(RBA.at[r, d, s - 1], rr_s.at[r, d, s - 1], rr_r.at[r, d, s - 1])
            p[...] = (p[...].astype(F32) + RBA[r, d, s - 1].astype(F32)).astype(BF)
        send(p, RBA.at[r, d, s], rr_s.at[r, d, s], rr_r.at[r, d, s], c, y * 8 + zz(step_dir[r]))

    def back_x(o):
        for d in range(1, 4):
            send(
                YY.at[zz(o), rows_b(xx(d), NR)], XRB.at[o % 8, d - 1],
                rx2_s.at[o % 8, d - 1], rx2_r.at[o % 8, d - 1], 2 * xx(d) + k, e,
            )

    def back_x_sum(o):
        acc = YY[zz(o), rows_b(x, NR), :].astype(F32)
        for d in range(1, 4):
            arrive(XRB.at[o % 8, d - 1], rx2_s.at[o % 8, d - 1], rx2_r.at[o % 8, d - 1])
            acc = acc + XRB[o % 8, d - 1].astype(F32)
        return acc

    def back_ring_b(r, s):
        o = step_dir[r] * (HOPB[r] - s)
        acc = back_x_sum(o)
        if s:
            arrive(RBB.at[r, s - 1], rb_s.at[r, s - 1], rb_r.at[r, s - 1])
            acc = acc + RBB[r, s - 1].astype(F32)
        p = YY.at[zz(o), rows_b(x, NR)]
        p[...] = acc.astype(BF)
        send(p, RBB.at[r, s], rb_s.at[r, s], rb_r.at[r, s], c, y * 8 + zz(step_dir[r]))

    for o in (4, 3, -3, -2, 2, -1, 1, 0):
        down(o)
        for r in range(2):
            for d in range(4):
                if (step_dir[r] * HOPS[r][d] - o) % 8 == 0:
                    back_ring(r, d, 0)
        back_x(o)
    for s in range(1, 4):
        for d in (2, 1, 3, 0):
            for r in range(2):
                if s < HOPS[r][d]:
                    back_ring(r, d, s)
        for r in range(2):
            back_ring_b(r, s - 1)
    for d in (2, 1, 3, 0):
        acc = YY[z, rows_a(xx(d), NR), :].astype(F32)
        for r in range(2):
            s = HOPS[r][d] - 1
            arrive(RBA.at[r, d, s], rr_s.at[r, d, s], rr_r.at[r, d, s])
            acc = acc + RBA[r, d, s].astype(F32)
        if d:
            p = YY.at[z, rows_a(xx(d), NR)]
            p[...] = acc.astype(BF)
            send(p, XRA.at[d - 1], ra_s.at[d - 1], ra_r.at[d - 1], 2 * xx(d) + k, e)
        else:
            YS[:NR, :] = acc
    back_ring_b(0, 3)
    acc = back_x_sum(0)
    for r in range(2):
        s = HOPB[r] - 1
        arrive(RBB.at[r, s], rb_s.at[r, s], rb_r.at[r, s])
        acc = acc + RBB[r, s].astype(F32)
    YS[NR:, :] = acc
    acc = YS[:NR, :]
    for d in range(1, 4):
        arrive(XRA.at[d - 1], ra_s.at[d - 1], ra_r.at[d - 1])
        acc = acc + XRA[d - 1].astype(F32)
    YS[:NR, :] = acc

    first = (y == 0).astype(F32)
    target = 2 * b
    for kc in range(2):
        got = nn(PT[kc], YS[kc * CAP:(kc + 1) * CAP, :].astype(BF))
        got = got * GC[kc, :, 0:1] + first * MID[kc]
        for j in range(2):
            FS[kc * 2 + j] = got[:, j * OUT:(j + 1) * OUT].astype(BF)
            dc, de = 2 * x + kc, target + j
            is_me = (k == kc) & (de == e)

            @pl.when(is_me)
            def _(i=kc * 2 + j):
                FR[y] = FS[i]

            @pl.when(jnp.logical_not(is_me))
            def _(i=kc * 2 + j, dc=dc, de=de):
                send(FS.at[i], FR.at[y], fn_s.at[i], fn_r.at[y], dc, de, False)

    for yy in range(4):
        @pl.when(jnp.logical_not(src_mine & (y == yy)))
        def _(yy=yy):
            arrive(FR.at[yy], fn_s.at[yy], fn_r.at[yy])
    acc = FR[0].astype(F32)
    for yy in range(1, 4):
        acc = acc + FR[yy].astype(F32)
    out_ref[...] = acc.astype(BF)

    def left(src, ss):
        pltpu.make_async_remote_copy(
            src_ref=src, dst_ref=src, send_sem=ss, recv_sem=ss,
            device_id=(c, e), device_id_type=MESH,
        ).wait_send()

    for cp in pend:
        cp.wait_send()
    for d in range(1, 4):
        @pl.when(x + d < 4)
        def _(d=d):
            left(TC, tt_s.at[d])
            left(LC, st_s.at[d])
    for kc in range(2):
        @pl.when(k != kc)
        def _(kc=kc):
            left(QQ.at[:, cols(kc * 8 + pos(z), FY)], a2_s.at[kc, 0])
            left(PZ.at[:, cols(kc * 8 + pos(z), FZ)], z1_s.at[kc, 0])
        for j in range(2):
            @pl.when(jnp.logical_not((k == kc) & (target + j == e)))
            def _(i=kc * 2 + j):
                left(FS.at[i], fn_s.at[i])


def local(tok, q, kk, v, ld, inc, ag, wo, fg, ro, ids, wi, wd):
    vm = lambda *s, t=BF: pltpu.VMEM(s, t)
    dma = lambda *s: pltpu.SemaphoreType.DMA(s)
    inside = pl.BlockSpec(memory_space=pltpu.VMEM)
    outside = pl.BlockSpec(memory_space=pl.ANY)
    scratch = [
        vm(256, D), vm(2, 2, SL, HALF), vm(2, SL, HALF), vm(2, T, FB), vm(2, 8, T, t=F32),
        vm(2, HD, HD, t=F32), vm(2, HD, HD), vm(8, T, t=F32), vm(4, HD, HD), vm(4, 8, T, t=F32),
        vm(2, HD, HD, t=F32), vm(HD, HD, t=F32), vm(HD, HD), vm(8, T, t=F32),
        vm(2, T, HD, t=F32), vm(2, T, HD, t=F32), vm(8, T, t=F32),
        vm(T, 2 * HD), vm(T, DY), vm(T, D - DY), vm(3, 32, DY), vm(32, DY), vm(2, 8, 32, FY),
        vm(2, 8, T, FZ), vm(2, T, FZ), vm(3, 2, 32, FZ), vm(4, 2, 32, FB),
        vm(2, T, FB, t=F32),
        vm(2, T, T, t=F32), vm(2, T, CAP), vm(2, T, T, t=F32), vm(16, 8, 2 * T, t=F32), vm(8, 2 * T, t=F32), vm(4, 8, 2 * T, t=F32), vm(8, 8 * CAP, FB),
        vm(4, 8 * CAP, SL, t=F32), vm(2, 8 * CAP, SL), vm(2, 8 * CAP, SL), vm(2, 8 * CAP, SL),
        vm(8, 8 * CAP, FB), vm(2, 4, 4, NR, FB), vm(2, 4, 160 - NR, FB), vm(3, NR, FB), vm(8, 3, 160 - NR, FB),
        vm(160, FB, t=F32), vm(4, T, OUT), vm(4, T, OUT),
        dma(5), dma(4), dma(4), dma(4), dma(4), dma(5), dma(5),
        dma(6), dma(6), dma(2, 8), dma(2, 8), dma(3), dma(3), dma(2, 8), dma(2, 8), dma(3), dma(3), dma(16), dma(16), dma(3), dma(3),
        dma(5), dma(5), dma(3), dma(3), dma(2, 4, 4), dma(2, 4, 4), dma(2, 4), dma(2, 4), dma(8, 3), dma(8, 3),
        dma(3), dma(3), dma(2, 4, 4), dma(2, 4, 4), dma(2, 4), dma(2, 4), dma(8, 3), dma(8, 3), dma(4), dma(4),
    ]
    return pl.pallas_call(
        kernel,
        out_shape=jax.ShapeDtypeStruct((T, OUT), BF),
        in_specs=[
            outside, inside, inside, inside, inside, inside, inside,
            outside, inside, inside, inside, outside, outside,
        ],
        out_specs=inside,
        scratch_shapes=scratch,
        compiler_params=pltpu.CompilerParams(
            collective_id=0, has_side_effects=True, vmem_limit_bytes=56 * 2**20
        ),
        cost_estimate=pl.CostEstimate(flops=4 * 10**9, bytes_accessed=10**7, transcendentals=10**5),
    )(tok, q, kk, v, ld, inc, ag.reshape(2, HD), wo, fg.reshape(D // 128, 128), ro.T, ids.T, wi, wd)


def solution(mesh):
    return jax.shard_map(
        local,
        mesh=mesh,
        in_specs=(
            P("ctx", None),
            P("ctx", "exp"),
            P("ctx", "exp"),
            P("ctx", "exp"),
            P("exp", "ctx"),
            P("exp", None, None),
            P("exp"),
            P("exp", None),
            P(),
            P(),
            P("ctx", None),
            P(None, ("exp", "ctx"), None),
            P(("exp", "ctx"), None),
        ),
        out_specs=P("ctx", "exp"),
        check_vma=False,
    )
```

```python
import functools

import jax
import jax.numpy as jnp
from jax import lax
from jax.experimental import pallas as pl
from jax.experimental.pallas import tpu as pltpu
from jax.sharding import PartitionSpec as P

MESH = pl.DeviceIdType.MESH
HI = lax.Precision.HIGHEST
F32 = jnp.float32
BF = jnp.bfloat16
EPS = 1e-06

D = 6144
T = 128
HD = 128
CAP = 80
SL = 144
HALF = D // 2
FB = HALF // 8
OUT = D // 32
FZ = 128
FY = FB - FZ
DY = 16 * FY

HOPS = ((4, 4, 3, 3), (3, 3, 4, 4))
HOPB = (4, 3)
NG = 64
NR = 64


def nt(a, b, precision=None):
    return lax.dot_general(
        a, b, (((1,), (1,)), ((), ())), preferred_element_type=F32, precision=precision
    )


def nn(a, b, precision=None):
    return jnp.dot(a, b, preferred_element_type=F32, precision=precision)


def iota2(shape, dim):
    return lax.broadcasted_iota(jnp.int32, shape, dim)


def kernel(
    tok_ref,
    q_ref,
    k_ref,
    v_ref,
    ld_ref,
    inc_ref,
    ag_ref,
    wo_ref,
    fg_ref,
    ro_ref,
    ids_ref,
    wi_ref,
    wd_ref,
    out_ref,
    WO, WI, WD, TK, IDS,
    LF, LS, TS, LB, TB, ST, SO, LC, TC, IN, QS, WR,
    AH, PP, PZ, A1R, QQ, A2R, Z1R, ZQ, Z2R, A3R, MID,
    PL, PT, GC, SR, LG, RX, XG, ACC, PS, PR, HID,
    YY, RBA, RBB, XRA, XRB, YS, FS, FR,
    loc, sib_s, sib_r, st_s, st_r, tt_s, tt_r,
    a1_s, a1_r, z1_s, z1_r, z2_s, z2_r, a2_s, a2_r, a3_s, a3_r, sx_s, sx_r, rx_s, rx_r,
    pr_s, pr_r, ax_s, ax_r, ar_s, ar_r, br_s, br_r, bx_s, bx_r,
    ra_s, ra_r, rr_s, rr_r, rb_s, rb_r, rx2_s, rx2_r, fn_s, fn_r,
):
    c = lax.axis_index("ctx")
    e = lax.axis_index("exp")
    x, k = c // 2, lax.rem(c, 2)
    y, z = e // 8, lax.rem(e, 8)

    def pos(zs):
        return lax.rem(zs, 2) * 4 + zs // 2

    b = k * 8 + pos(z)
    pend = []

    def xx(d):
        return lax.rem(x + (d + 8), 4)

    def yv(d):
        return lax.rem(y + (d + 8), 4)

    def zz(o):
        return lax.rem(z + (o + 16), 8)

    def send(src, dst, ss, rs, dc, de, keep=True):
        cp = pltpu.make_async_remote_copy(
            src_ref=src, dst_ref=dst, send_sem=ss, recv_sem=rs,
            device_id=(dc, de), device_id_type=MESH,
        )
        cp.start()
        if keep:
            pend.append(cp)
        return cp

    def arrive(dst, ss, rs):
        pltpu.make_async_remote_copy(
            src_ref=dst, dst_ref=dst, send_sem=ss, recv_sem=rs,
            device_id=(c, e), device_id_type=MESH,
        ).wait_recv()

    def cols(i, n):
        return pl.ds(pl.multiple_of(i * n, 128), n)

    bar = pltpu.get_barrier_semaphore()

    def hello(dc, de):
        pl.semaphore_signal(bar, inc=1, device_id=(dc, de), device_id_type=MESH)

    sibling = 2 * x + (1 - k)
    hello(sibling, e)
    for d in range(1, 4):
        hello(2 * xx(d) + k, e)
    for d in range(1, 4):
        hello(c, yv(d) * 8 + z)
    for o in (4, 3, 5, 2, 6, 1, 7):
        hello(c, y * 8 + zz(o))
        hello(sibling, y * 8 + zz(o))
    src_b = e // 2
    src_k, src_p = src_b // 8, lax.rem(src_b, 8)
    src_z = 2 * lax.rem(src_p, 4) + src_p // 4
    src_mine = (src_k == k) & (src_z == z)
    for yy in range(4):
        @pl.when(jnp.logical_not(src_mine & (y == yy)))
        def _(yy=yy):
            hello(2 * x + src_k, yy * 8 + src_z)
    lc_wo = pltpu.make_async_copy(wo_ref, WO, loc.at[0])
    lc_wo.start()
    lc_tk = pltpu.make_async_copy(tok_ref.at[:, cols(b, FB)], TK.at[k], loc.at[1])
    lc_tk.start()

    row_i = iota2((T, T), 0)
    col_i = iota2((T, T), 1)
    lower = row_i >= col_i
    scale = HD ** (-0.5)
    cums = []
    for h in range(2):
        hs = slice(h * HD, (h + 1) * HD)
        ld = ld_ref[h:h + 1, :]
        cum = jnp.sum(jnp.where(lower, ld, 0.0), axis=1, keepdims=True)
        tot = jnp.sum(ld, axis=1, keepdims=True)
        cums.append(cum)
        ks = k_ref[:, hs].astype(F32) * jnp.exp(tot - cum)
        LF[h] = nn(ks.T, v_ref[:, hs].astype(F32), HI)
        LS[h] = LF[h].astype(BF)
        TS[h:h + 1, :] = jnp.broadcast_to(tot, (1, T))
    TS[2:, :] = jnp.zeros((6, T), F32)
    IDS[k, 0:2, :] = ids_ref[...].astype(F32)
    IDS[k, 2:8, :] = jnp.zeros((6, T), F32)

    pl.semaphore_wait(bar, 25 - (src_mine).astype(jnp.int32))

    send(TS, TB.at[0], tt_s.at[0], tt_r.at[0], sibling, e)
    send(LS.at[1 - k], LB.at[0], st_s.at[0], st_r.at[0], sibling, e)
    ob = (1 - k) * 8 + pos(z)
    send(tok_ref.at[:, cols(ob, FB)], TK.at[k], sib_s.at[0], sib_r.at[0], sibling, e)
    send(IDS.at[k], IDS.at[k], sib_s.at[1], sib_r.at[1], sibling, e)
    mine, other = cols(k, HALF), cols(1 - k, HALF)
    lc_wi = pltpu.make_async_copy(wi_ref.at[:, :, mine], WI.at[k], loc.at[3])
    lc_wi.start()
    lc_wd = pltpu.make_async_copy(wd_ref.at[:, mine], WD.at[k], loc.at[4])
    lc_wd.start()
    send(wi_ref.at[:, :, other], WI.at[k], sib_s.at[2], sib_r.at[2], sibling, e)
    send(wd_ref.at[:, other], WD.at[k], sib_s.at[3], sib_r.at[3], sibling, e)

    arrive(TB.at[0], tt_s.at[0], tt_r.at[0])
    arrive(LB.at[0], st_s.at[0], st_r.at[0])
    mine_l, other_l = LF[k], LB[0].astype(F32)
    mine_t, other_t = TS[pl.ds(k, 1), :], TB[0, pl.ds(k, 1), :]
    core0 = k == 0
    l0 = jnp.where(core0, mine_l, other_l)
    l1 = jnp.where(core0, other_l, mine_l)
    t0 = jnp.where(core0, mine_t, other_t)
    t1 = jnp.where(core0, other_t, mine_t)
    LC[...] = (jnp.exp(t1) * l0 + l1).astype(BF)
    TC[...] = jnp.broadcast_to(t0 + t1, (8, T))
    for d in range(1, 4):
        @pl.when(x + d < 4)
        def _(d=d):
            send(TC, TB.at[d], tt_s.at[d], tt_r.at[d], c + 2 * d, e, False)
            send(LC, LB.at[d], st_s.at[d], st_r.at[d], c + 2 * d, e, False)

    for h in range(2):
        hs = slice(h * HD, (h + 1) * HD)
        cum = cums[h]
        cb = jnp.broadcast_to(cum, (T, T))
        gap = jnp.where(lower, cb - cb.T, 0.0)
        weight = jnp.where(lower, jnp.exp(gap), 0.0)
        sc = nt(q_ref[:, hs], k_ref[:, hs]) * scale * weight
        IN[h] = nn(sc, v_ref[:, hs].astype(F32), HI)
        QS[h] = q_ref[:, hs].astype(F32) * (scale * jnp.exp(cum))

    ST[k] = jnp.zeros((HD, HD), F32)
    WR[...] = jnp.zeros_like(WR)
    for d in range(1, 4):
        @pl.when(x >= d)
        def _(d=d):
            arrive(TB.at[d], tt_s.at[d], tt_r.at[d])
            arrive(LB.at[d], st_s.at[d], st_r.at[d])
            ST[k] = ST[k] + jnp.exp(WR[0:1, :]) * LB[d].astype(F32)
            WR[...] = WR[...] + TB[d]
    start = ST[k] + jnp.exp(WR[0:1, :]) * inc_ref[k]
    after = jnp.exp(t0) * start + l0
    ST[k] = jnp.where(core0, start, after)
    SO[...] = jnp.where(core0, after, start)
    send(SO, ST.at[k], tt_s.at[4], tt_r.at[4], sibling, e)

    def finish(h):
        att = IN[h] + nn(QS[h], ST[h], HI)
        ms = jnp.mean(att * att, axis=1, keepdims=True)
        AH[:, pl.ds(pl.multiple_of(h * HD, HD), HD)] = (
            att * lax.rsqrt(ms + EPS) * ag_ref[pl.ds(h, 1), :]
        ).astype(BF)

    finish(k)
    arrive(ST.at[1 - k], tt_s.at[4], tt_r.at[4])
    finish(1 - k)

    lc_wo.wait()
    for kc in range(2):
        def project(i, carry, kc=kc):
            bl = kc * 8 + i
            r = nn(AH[...], WO[:, cols(bl, FB)]).astype(BF)
            PP[:, cols(bl, FY)] = r[:, :FY]
            PZ[:, cols(bl, FZ)] = r[:, FY:]
            return carry
        lax.fori_loop(0, 8, project, 0)
        cs = slice(kc * 8 * FY, (kc + 1) * 8 * FY)
        for d in (2, 1, 3):
            i = kc * 3 + d - 1
            send(
                PP.at[pl.ds(pl.multiple_of(yv(d) * 32, 32), 32), cs],
                A1R.at[d - 1, :, cs],
                a1_s.at[i], a1_r.at[i], c, yv(d) * 8 + z,
            )
        dest = 2 * x + kc
        for o in (4, 3, 5, 2, 6, 1, 7):
            send(
                PZ.at[:, cols(kc * 8 + pos(zz(o)), FZ)],
                Z1R.at[k, o], z1_s.at[kc, o], z1_r.at[k, o], dest, y * 8 + zz(o),
            )
        own = cols(kc * 8 + pos(z), FZ)

        @pl.when(k == kc)
        def _(own=own):
            Z1R[k, 0] = PZ[:, own]

        @pl.when(k != kc)
        def _(own=own, kc=kc, dest=dest):
            send(PZ.at[:, own], Z1R.at[k, 0], z1_s.at[kc, 0], z1_r.at[k, 0], dest, e, False)
    for kc in range(2):
        cs = slice(kc * 8 * FY, (kc + 1) * 8 * FY)
        for d in range(1, 4):
            i = kc * 3 + d - 1
            arrive(A1R.at[d - 1, :, cs], a1_s.at[i], a1_r.at[i])

        def add_y(i, carry, kc=kc):
            s = pl.ds(pl.multiple_of(kc * 8 * FY + i * 512, 128), 512)
            acc = PP[pl.ds(pl.multiple_of(y * 32, 32), 32), s].astype(F32)
            for d in range(3):
                acc = acc + A1R[d, :, s].astype(F32)
            QQ[:, s] = acc.astype(BF)
            return carry
        lax.fori_loop(0, 8 * FY // 512, add_y, 0)
        dest = 2 * x + kc
        for o in (4, 3, 5, 2, 6, 1, 7):
            send(
                QQ.at[:, cols(kc * 8 + pos(zz(o)), FY)],
                A2R.at[k, o], a2_s.at[kc, o], a2_r.at[k, o], dest, y * 8 + zz(o),
            )
        own = cols(kc * 8 + pos(z), FY)

        @pl.when(k == kc)
        def _(own=own):
            A2R[k, 0] = QQ[:, own]

        @pl.when(k != kc)
        def _(own=own, kc=kc, dest=dest):
            send(QQ.at[:, own], A2R.at[k, 0], a2_s.at[kc, 0], a2_r.at[k, 0], dest, e, False)

    for kc in range(2):
        @pl.when(k != kc)
        def _(kc=kc):
            arrive(Z1R.at[kc, 0], z1_s.at[kc, 0], z1_r.at[kc, 0])
        acc = Z1R[kc, 0].astype(F32)
        for o in range(1, 8):
            arrive(Z1R.at[kc, o], z1_s.at[kc, o], z1_r.at[kc, o])
            acc = acc + Z1R[kc, o].astype(F32)
        ZQ[kc] = acc.astype(BF)
    for d in (2, 1, 3):
        send(
            ZQ.at[:, pl.ds(pl.multiple_of(yv(d) * 32, 32), 32)], Z2R.at[d - 1],
            z2_s.at[d - 1], z2_r.at[d - 1], c, yv(d) * 8 + z,
        )
    for kc in range(2):
        @pl.when(k != kc)
        def _(kc=kc):
            arrive(A2R.at[kc, 0], a2_s.at[kc, 0], a2_r.at[kc, 0])
        acc = A2R[kc, 0].astype(F32)
        for o in range(1, 8):
            arrive(A2R.at[kc, o], a2_s.at[kc, o], a2_r.at[kc, o])
            acc = acc + A2R[kc, o].astype(F32)
        A3R[0, kc, :, :FY] = acc.astype(BF)
    acc = ZQ[:, pl.ds(pl.multiple_of(y * 32, 32), 32), :].astype(F32)
    for d in range(1, 4):
        arrive(Z2R.at[d - 1], z2_s.at[d - 1], z2_r.at[d - 1])
        acc = acc + Z2R[d - 1].astype(F32)
    A3R[0, :, :, FY:] = acc.astype(BF)
    for d in range(1, 4):
        send(A3R.at[0], A3R.at[d], a3_s.at[d - 1], a3_r.at[d - 1], c, yv(d) * 8 + z)

    arrive(IDS.at[1 - k], sib_s.at[1], sib_r.at[1])
    strict = (row_i < col_i).astype(BF)
    yf = y.astype(F32)
    for kc in range(2):
        mask = ((IDS[kc, 0:1, :] == yf) | (IDS[kc, 1:2, :] == yf)).astype(F32)
        before = nn(jnp.broadcast_to(mask, (8, T)).astype(BF), strict)[0:1, :]
        PL[kc] = jnp.where(
            (row_i.astype(F32) == before) & (row_i < CAP), mask, 0.0
        )

    lc_tk.wait()
    arrive(TK.at[1 - k], sib_s.at[0], sib_r.at[0])
    gain = jnp.concatenate([fg_ref[pl.ds(b * 3 + i, 1), :] for i in range(3)], axis=1)
    for d in range(4):
        if d:
            arrive(A3R.at[d], a3_s.at[d - 1], a3_r.at[d - 1])
        rows = pl.ds(pl.multiple_of(yv(-d) * 32, 32), 32)
        for kc in range(2):
            MID[kc, rows, :] = TK[kc, rows, :].astype(F32) + A3R[d, kc].astype(F32)

    def rows_a(i, n=NG):
        return pl.ds(pl.multiple_of(i * 160, 16), n)

    def rows_b(i, n=NG):
        return pl.ds(pl.multiple_of(i * 160 + n, 16), 160 - n)

    def slot_rows(i, kc):
        return pl.ds(pl.multiple_of(i * 160 + 80 * kc, 16), 80)

    def piece_a(zs, d):
        return XG.at[zs, rows_a(xx(-d))]

    def piece_b(zs, d):
        return XG.at[zs, rows_b(xx(-d))]

    step_dir = (1, -1)

    def alpha_ring(r, d, h):
        p = piece_a(zz(-step_dir[r] * (h - 1)), d)
        send(p, p, ar_s.at[r, d, h - 1], ar_r.at[r, d, h - 1], c, y * 8 + zz(step_dir[r]))

    def beta_ring(r, h):
        p = piece_b(zz(-step_dir[r] * (h - 1)), 0)
        send(p, p, br_s.at[r, h - 1], br_r.at[r, h - 1], c, y * 8 + zz(step_dir[r]))

    def beta_x(o):
        p = piece_b(zz(o), 0)
        for d in (2, 1, 3):
            send(p, p, bx_s.at[o % 8, d - 1], bx_r.at[o % 8, d - 1], 2 * xx(d) + k, e)

    def beta_x_wait(o):
        for d in range(1, 4):
            arrive(piece_b(zz(o), d), bx_s.at[o % 8, d - 1], bx_r.at[o % 8, d - 1])

    for kc in (1, 0):
        xg = (MID[kc] * gain).astype(BF)
        slots = nn(PL[kc, :CAP, :].astype(BF), xg).astype(BF)
        XG[z, slot_rows(x, kc), :] = slots
        if kc and NG >= 80:
            beta_ring(0, 1)
            beta_ring(1, 1)
    if NG < 80:
        beta_ring(0, 1)
        beta_ring(1, 1)
    pa = piece_a(z, 0)
    for d in range(1, 4):
        send(pa, pa, ax_s.at[d - 1], ax_r.at[d - 1], 2 * xx(d) + k, e)
    alpha_ring(0, 0, 1)
    alpha_ring(1, 0, 1)
    beta_x(0)
    lc_wi.wait()
    arrive(WI.at[1 - k], sib_s.at[2], sib_r.at[2])

    def ffn_in(o, first=False):
        zs = zz(o)
        ws = cols(pos(zs), FB)

        def body(i, carry):
            rows = pl.ds(pl.multiple_of(i * 160, 16), 160)
            xb = XG[zs, rows, :]
            for q in range(4):
                r = nt(xb, WI[q // 2, q % 2, :, ws])
                if first:
                    ACC[q, rows, :] = r
                else:
                    ACC[q, rows, :] = ACC[q, rows, :] + r
            return carry
        lax.fori_loop(0, 4, body, 0)

    for h in range(1, 5):
        for r in range(2):
            if h <= HOPB[r]:
                arrive(piece_b(zz(-step_dir[r] * h), 0), br_s.at[r, h - 1], br_r.at[r, h - 1])
                if h < HOPB[r]:
                    beta_ring(r, h + 1)
                beta_x(-step_dir[r] * h)
        for d in range(4):
            if h == 1 and d:
                arrive(piece_a(z, d), ax_s.at[d - 1], ax_r.at[d - 1])
                alpha_ring(0, d, 1)
                alpha_ring(1, d, 1)
        for d in range(4):
            for r in range(2):
                if h <= HOPS[r][d]:
                    arrive(
                        piece_a(zz(-step_dir[r] * h), d),
                        ar_s.at[r, d, h - 1], ar_r.at[r, d, h - 1],
                    )
                    if h < HOPS[r][d]:
                        alpha_ring(r, d, h + 1)
        if h == 1:
            beta_x_wait(0)
            ffn_in(0, True)
        else:
            for o in (h - 1, 1 - h):
                beta_x_wait(o)
                ffn_in(o)
        if h == 2:
            router = ro_ref[:, cols(b, FB)]
            for kc in range(2):
                m = MID[kc]
                ts = slice(kc * T, (kc + 1) * T)
                SR[0, 0:4, ts] = nt(router, (m * gain).astype(BF))
                square = jnp.sum(m * m, axis=1, keepdims=True)
                SR[0, 4:8, ts] = jnp.broadcast_to(square, (T, T)).T[0:4, :]
            for o in range(16):
                if o:
                    dk = o // 8
                    send(
                        SR.at[0], SR.at[o], sx_s.at[o], sx_r.at[o],
                        sibling if dk else c, y * 8 + zz(o % 8),
                    )

        if h == 4:
            for o in range(1, 16):
                arrive(SR.at[o], sx_s.at[o], sx_r.at[o])
            tot = SR[0]
            for o in range(1, 16):
                tot = tot + SR[o]
            rstd = lax.rsqrt(tot[4:5, :] / D + EPS)
            LG[...] = tot * rstd
            rs = jnp.concatenate(
                [
                    nt(jnp.broadcast_to(rstd[:, kc * T:(kc + 1) * T], (8, T)), PL[kc], HI)
                    for kc in range(2)
                ],
                axis=1,
            )
            RX[0] = rs
            for d in range(1, 4):
                send(RX.at[0], RX.at[d], rx_s.at[d - 1], rx_r.at[d - 1], 2 * xx(d) + k, e)
    beta_x_wait(-4)
    ws4 = cols(pos(zz(4)), FB)

    for g in range(2):
        def last(i, carry, g=g):
            rows = pl.ds(pl.multiple_of(i * 160, 16), 160)
            r = nt(XG[zz(4), rows, :], WI[1 - k, g, :, ws4])
            PS[g, rows, :] = (ACC[2 * (1 - k) + g, rows, :] + r).astype(BF)
            return carry
        lax.fori_loop(0, 4, last, 0)
        send(PS.at[g], PR.at[g], pr_s.at[5 * g], pr_r.at[5 * g], sibling, e)

    def last_own(i, carry):
        rows = pl.ds(pl.multiple_of(i * 160, 16), 160)
        for g in range(2):
            r = nt(XG[zz(4), rows, :], WI[k, g, :, ws4])
            ACC[2 * k + g, rows, :] = ACC[2 * k + g, rows, :] + r
        return carry
    lax.fori_loop(0, 4, last_own, 0)
    for kc in range(2):
        sg = 1.0 / (1.0 + jnp.exp(-LG[:, kc * T:(kc + 1) * T]))
        i0, i1 = IDS[kc, 0:1, :], IDS[kc, 1:2, :]
        den = jnp.zeros((1, T), F32)
        num = jnp.zeros((1, T), F32)
        for j in range(4):
            hit = ((i0 == j) | (i1 == j)).astype(F32) * sg[j:j + 1, :]
            den = den + hit
            num = num + jnp.where(y == j, hit, 0.0)
        GC[kc] = jnp.broadcast_to(num / den, (T, T)).T
        PT[kc] = PL[kc].T[:, :CAP].astype(BF)
    for d in range(1, 4):
        arrive(RX.at[d], rx_s.at[d - 1], rx_r.at[d - 1])
    lc_wd.wait()
    arrive(WD.at[1 - k], sib_s.at[3], sib_r.at[3])
    for g in range(2):
        arrive(PR.at[g], pr_s.at[5 * g], pr_r.at[5 * g])
    for d in range(4):
        for kc in range(2):
            rs = RX[d, 0:1, kc * T:(kc + 1) * T]
            col = jnp.broadcast_to(rs, (T, T)).T[:CAP, 0:1]
            rows = slot_rows(xx(-d), kc)
            g = (ACC[2 * k, rows, :] + PR[0, rows, :].astype(F32)) * col
            u = (ACC[2 * k + 1, rows, :] + PR[1, rows, :].astype(F32)) * col
            HID[k, rows, :] = (g / (1.0 + jnp.exp(-g)) * u).astype(BF)
        part = HID.at[k, pl.ds(pl.multiple_of(xx(-d) * 160, 16), 160)]
        send(part, part, pr_s.at[1 + d], pr_r.at[1 + d], sibling, e)
    for d in range(4):
        part = HID.at[1 - k, pl.ds(pl.multiple_of(xx(-d) * 160, 16), 160)]
        arrive(part, pr_s.at[1 + d], pr_r.at[1 + d])

    def down(o):
        zs = zz(o)
        ws = cols(pos(zs), FB)

        def body(i, carry):
            rows = pl.ds(pl.multiple_of(i * 160, 16), 160)
            r = nn(HID[0, rows, :], WD[0, :, ws]) + nn(HID[1, rows, :], WD[1, :, ws])
            YY[zs, rows, :] = r.astype(BF)
            return carry
        lax.fori_loop(0, 4, body, 0)

    def back_ring(r, d, s):
        hops = HOPS[r][d]
        zs = zz(step_dir[r] * (hops - s))
        p = YY.at[zs, rows_a(xx(d), NR)]
        if s:
            arrive(RBA.at[r, d, s - 1], rr_s.at[r, d, s - 1], rr_r.at[r, d, s - 1])
            p[...] = (p[...].astype(F32) + RBA[r, d, s - 1].astype(F32)).astype(BF)
        send(p, RBA.at[r, d, s], rr_s.at[r, d, s], rr_r.at[r, d, s], c, y * 8 + zz(step_dir[r]))

    def back_x(o):
        for d in range(1, 4):
            send(
                YY.at[zz(o), rows_b(xx(d), NR)], XRB.at[o % 8, d - 1],
                rx2_s.at[o % 8, d - 1], rx2_r.at[o % 8, d - 1], 2 * xx(d) + k, e,
            )

    def back_x_sum(o):
        acc = YY[zz(o), rows_b(x, NR), :].astype(F32)
        for d in range(1, 4):
            arrive(XRB.at[o % 8, d - 1], rx2_s.at[o % 8, d - 1], rx2_r.at[o % 8, d - 1])
            acc = acc + XRB[o % 8, d - 1].astype(F32)
        return acc

    def back_ring_b(r, s):
        o = step_dir[r] * (HOPB[r] - s)
        acc = back_x_sum(o)
        if s:
            arrive(RBB.at[r, s - 1], rb_s.at[r, s - 1], rb_r.at[r, s - 1])
            acc = acc + RBB[r, s - 1].astype(F32)
        p = YY.at[zz(o), rows_b(x, NR)]
        p[...] = acc.astype(BF)
        send(p, RBB.at[r, s], rb_s.at[r, s], rb_r.at[r, s], c, y * 8 + zz(step_dir[r]))

    for o in (4, 3, -3, -2, 2, -1, 1, 0):
        down(o)
        for r in range(2):
            for d in range(4):
                if (step_dir[r] * HOPS[r][d] - o) % 8 == 0:
                    back_ring(r, d, 0)
        back_x(o)
    for s in range(1, 4):
        for d in (2, 1, 3, 0):
            for r in range(2):
                if s < HOPS[r][d]:
                    back_ring(r, d, s)
        for r in range(2):
            back_ring_b(r, s - 1)
    for d in (2, 1, 3, 0):
        acc = YY[z, rows_a(xx(d), NR), :].astype(F32)
        for r in range(2):
            s = HOPS[r][d] - 1
            arrive(RBA.at[r, d, s], rr_s.at[r, d, s], rr_r.at[r, d, s])
            acc = acc + RBA[r, d, s].astype(F32)
        if d:
            p = YY.at[z, rows_a(xx(d), NR)]
            p[...] = acc.astype(BF)
            send(p, XRA.at[d - 1], ra_s.at[d - 1], ra_r.at[d - 1], 2 * xx(d) + k, e)
        else:
            YS[:NR, :] = acc
    back_ring_b(0, 3)
    acc = back_x_sum(0)
    for r in range(2):
        s = HOPB[r] - 1
        arrive(RBB.at[r, s], rb_s.at[r, s], rb_r.at[r, s])
        acc = acc + RBB[r, s].astype(F32)
    YS[NR:, :] = acc
    acc = YS[:NR, :]
    for d in range(1, 4):
        arrive(XRA.at[d - 1], ra_s.at[d - 1], ra_r.at[d - 1])
        acc = acc + XRA[d - 1].astype(F32)
    YS[:NR, :] = acc

    first = (y == 0).astype(F32)
    target = 2 * b
    for kc in range(2):
        got = nn(PT[kc], YS[kc * CAP:(kc + 1) * CAP, :].astype(BF))
        got = got * GC[kc, :, 0:1] + first * MID[kc]
        for j in range(2):
            FS[kc * 2 + j] = got[:, j * OUT:(j + 1) * OUT].astype(BF)
            dc, de = 2 * x + kc, target + j
            is_me = (k == kc) & (de == e)

            @pl.when(is_me)
            def _(i=kc * 2 + j):
                FR[y] = FS[i]

            @pl.when(jnp.logical_not(is_me))
            def _(i=kc * 2 + j, dc=dc, de=de):
                send(FS.at[i], FR.at[y], fn_s.at[i], fn_r.at[y], dc, de, False)

    for yy in range(4):
        @pl.when(jnp.logical_not(src_mine & (y == yy)))
        def _(yy=yy):
            arrive(FR.at[yy], fn_s.at[yy], fn_r.at[yy])
    acc = FR[0].astype(F32)
    for yy in range(1, 4):
        acc = acc + FR[yy].astype(F32)
    out_ref[...] = acc.astype(BF)

    def left(src, ss):
        pltpu.make_async_remote_copy(
            src_ref=src, dst_ref=src, send_sem=ss, recv_sem=ss,
            device_id=(c, e), device_id_type=MESH,
        ).wait_send()

    for cp in pend:
        cp.wait_send()
    for d in range(1, 4):
        @pl.when(x + d < 4)
        def _(d=d):
            left(TC, tt_s.at[d])
            left(LC, st_s.at[d])
    for kc in range(2):
        @pl.when(k != kc)
        def _(kc=kc):
            left(QQ.at[:, cols(kc * 8 + pos(z), FY)], a2_s.at[kc, 0])
            left(PZ.at[:, cols(kc * 8 + pos(z), FZ)], z1_s.at[kc, 0])
        for j in range(2):
            @pl.when(jnp.logical_not((k == kc) & (target + j == e)))
            def _(i=kc * 2 + j):
                left(FS.at[i], fn_s.at[i])


def local(tok, q, kk, v, ld, inc, ag, wo, fg, ro, ids, wi, wd):
    vm = lambda *s, t=BF: pltpu.VMEM(s, t)
    dma = lambda *s: pltpu.SemaphoreType.DMA(s)
    inside = pl.BlockSpec(memory_space=pltpu.VMEM)
    outside = pl.BlockSpec(memory_space=pl.ANY)
    scratch = [
        vm(256, D), vm(2, 2, SL, HALF), vm(2, SL, HALF), vm(2, T, FB), vm(2, 8, T, t=F32),
        vm(2, HD, HD, t=F32), vm(2, HD, HD), vm(8, T, t=F32), vm(4, HD, HD), vm(4, 8, T, t=F32),
        vm(2, HD, HD, t=F32), vm(HD, HD, t=F32), vm(HD, HD), vm(8, T, t=F32),
        vm(2, T, HD, t=F32), vm(2, T, HD, t=F32), vm(8, T, t=F32),
        vm(T, 2 * HD), vm(T, DY), vm(T, D - DY), vm(3, 32, DY), vm(32, DY), vm(2, 8, 32, FY),
        vm(2, 8, T, FZ), vm(2, T, FZ), vm(3, 2, 32, FZ), vm(4, 2, 32, FB),
        vm(2, T, FB, t=F32),
        vm(2, T, T, t=F32), vm(2, T, CAP), vm(2, T, T, t=F32), vm(16, 8, 2 * T, t=F32), vm(8, 2 * T, t=F32), vm(4, 8, 2 * T, t=F32), vm(8, 8 * CAP, FB),
        vm(4, 8 * CAP, SL, t=F32), vm(2, 8 * CAP, SL), vm(2, 8 * CAP, SL), vm(2, 8 * CAP, SL),
        vm(8, 8 * CAP, FB), vm(2, 4, 4, NR, FB), vm(2, 4, 160 - NR, FB), vm(3, NR, FB), vm(8, 3, 160 - NR, FB),
        vm(160, FB, t=F32), vm(4, T, OUT), vm(4, T, OUT),
        dma(5), dma(4), dma(4), dma(4), dma(4), dma(5), dma(5),
        dma(6), dma(6), dma(2, 8), dma(2, 8), dma(3), dma(3), dma(2, 8), dma(2, 8), dma(3), dma(3), dma(16), dma(16), dma(3), dma(3),
        dma(6), dma(6), dma(3), dma(3), dma(2, 4, 4), dma(2, 4, 4), dma(2, 4), dma(2, 4), dma(8, 3), dma(8, 3),
        dma(3), dma(3), dma(2, 4, 4), dma(2, 4, 4), dma(2, 4), dma(2, 4), dma(8, 3), dma(8, 3), dma(4), dma(4),
    ]
    return pl.pallas_call(
        kernel,
        out_shape=jax.ShapeDtypeStruct((T, OUT), BF),
        in_specs=[
            outside, inside, inside, inside, inside, inside, inside,
            outside, inside, inside, inside, outside, outside,
        ],
        out_specs=inside,
        scratch_shapes=scratch,
        compiler_params=pltpu.CompilerParams(
            collective_id=0, has_side_effects=True, vmem_limit_bytes=56 * 2**20
        ),
        cost_estimate=pl.CostEstimate(flops=4 * 10**9, bytes_accessed=10**7, transcendentals=10**5),
    )(tok, q, kk, v, ld, inc, ag.reshape(2, HD), wo, fg.reshape(D // 128, 128), ro.T, ids.T, wi, wd)


def solution(mesh):
    return jax.shard_map(
        local,
        mesh=mesh,
        in_specs=(
            P("ctx", None),
            P("ctx", "exp"),
            P("ctx", "exp"),
            P("ctx", "exp"),
            P("exp", "ctx"),
            P("exp", None, None),
            P("exp"),
            P("exp", None),
            P(),
            P(),
            P("ctx", None),
            P(None, ("exp", "ctx"), None),
            P(("exp", "ctx"), None),
        ),
        out_specs=P("ctx", "exp"),
        check_vma=False,
    )
```
